512 devices in a mesh: tile: 16 (over x, z_lo), fsdp: 32 (over y, z_hi, core).
Axes of the slice: x: 4, y: 8, z: 8 (z_hi: 2, z_lo: 4; z = z_hi * 4 + z_lo), core: 2. Of those that a mesh axis runs over, the one named last changes fastest.
Arguments:
- tokens: bfloat16 [32, 12, 256, 4096], P('fsdp', None, 'tile'), may hold values from -6 to 6
- w_qkv: bfloat16 [4096, 384], P('fsdp'), may hold values from -4 to 4
- w_out: bfloat16 [128, 4096], P(None, 'fsdp'), may hold values from -0.5 to 0.5
- band: int32 [16, 2], P('tile'), may hold values from 1 to 2, as said below
- cotangent: bfloat16 [32, 12, 256, 4096], P('fsdp', None, 'tile'), may hold values from -6 to 6
Outputs:
- d_tokens: bfloat16 [32, 12, 256, 4096], P('fsdp', None, 'tile')
- grad_qkv: float32 [4096, 384], P('fsdp')
- grad_out: float32 [128, 4096], P(None, 'fsdp')
The draws below stay inside these ranges and needn't reach their ends.
Inputs may be any that keep to these rules, and one draw needn't show every extreme that they name: Every entry is the width of an intersection band in longitude patch columns.
All inputs are finite; a program needn't handle non-finite values.
Results may differ from the reference program's by a relative error of at most 0.03.
Values may be sent and summed in bfloat16 or wider, within the bound.
No kernel may reach another device: no remote copies, remote signals or barrier semaphores. Data moves between devices by JAX's collectives and lax.ppermute only.
A program may use at most 64 MiB of HBM per device.

```python
import jax
import jax.numpy as jnp
from jax import lax

D = 4096
HD = 128
HALO = 2
LAT = 12
LON_DEV = 16
TILES = 16
SAMPLES = 32
LON = 256
N_TILE = 16


def draw_band(key, part):
    key = jax.random.fold_in(key, 7)
    key_one, key_two, key_three, key_four = jax.random.split(key, 4)
    widths = jax.random.randint(key_one, (TILES, 2), 1, HALO + 1)
    first_tile = jax.random.randint(key_two, (), 0, TILES)
    second_tile = (first_tile + 1 + jax.random.randint(key_three, (), 0, TILES - 1)) % TILES
    which_side = jax.random.randint(key_four, (), 0, 2)
    widths = widths.at[first_tile, which_side].set(HALO)
    widths = widths.at[second_tile, 1 - which_side].set(1)
    return widths.astype(jnp.int32)


def draw_w_qkv(key, part):
    key = jax.random.fold_in(key, 13)
    key_one = jax.random.fold_in(key, 0)
    stacked = jax.random.normal(key_one, (D, 3 * HD), jnp.float32) * D ** (-0.5)
    stacked = jnp.clip(stacked, -4.0, 4.0)
    return stacked.astype(jnp.bfloat16)


def with_spikes(result, rng, source, target, parts, factor):
    def block_of(dim):
        return (jnp.arange(result.shape[dim]) // (result.shape[dim] // parts)).reshape((-1,) + (1,) * (result.ndim - 1 - dim))

    near = jax.random.permutation(rng, parts)[block_of(target)]
    far = (block_of(target) + parts // 2) % parts
    return jnp.where((block_of(source) == near) | (block_of(source) == far), factor * result, result)


def block_scale(rng, dims, cuts, least, top_value):
    level = 1.0
    for dim, blocks in cuts:
        heights = jax.random.uniform(jax.random.fold_in(jax.random.fold_in(rng, 6), dim), (blocks,), jnp.float32, least / len(cuts), top_value / len(cuts))
        level = level * jnp.repeat(jnp.exp(heights), dims[dim] // blocks).reshape((-1,) + (1,) * (len(dims) - 1 - dim))
    return level


def normal_values(key, dims, scale, bound, pieces=(), held_as=jnp.bfloat16):
    drawn = jax.random.normal(key, dims, jnp.float32) * scale
    if len(pieces) > 0:
        drawn = block_scale(key, dims, pieces, -0.22, 0.18) * drawn
    return jnp.clip(drawn, min=-bound, max=bound).astype(held_as)


def gaussian_with(stream_key, shape, width, bound, shards, heavy, dtype=jnp.bfloat16):
    result = width * jax.random.normal(stream_key, shape, jnp.float32)
    if shards:
        result = result * block_scale(stream_key, shape, shards, -0.22, 0.18)
    return jnp.clip(with_spikes(result, jax.random.fold_in(stream_key, 3), *heavy), -bound, bound).astype(dtype)


def setup_inputs(seed: int = 0) -> dict:
    keys = jax.random.split(jax.random.key(seed), 6)
    tokens = gaussian_with(keys[0], (SAMPLES, LAT, LON, D), 1.0, 6.0, ((0, 32), (2, 16)), (0, 3, 32, 2.75))
    w_qkv = draw_w_qkv(jax.random.fold_in(keys[5], 71), 0)
    w_out = normal_values(keys[2], (HD, D), HD ** -0.5, 0.5, ((1, 32),))
    band = draw_band(jax.random.fold_in(keys[5], 71), 0)
    cotangent = gaussian_with(keys[4], (SAMPLES, LAT, LON, D), 1.0, 6.0, ((0, 32), (2, 16)), (0, 3, 32, 2.75))
    return {"tokens": tokens, "w_qkv": w_qkv, "w_out": w_out, "band": band, "cotangent": cotangent}


EPS = 1e-05

def reference(tokens, w_qkv, w_out, band, cotangent):
    samples = tokens.shape[0]
    ext_cols = LON_DEV + 2 * HALO
    tok_grid = tokens.reshape(samples, LAT, N_TILE, LON_DEV, D).transpose(0, 2, 1, 3, 4)
    grad_grid = cotangent.reshape(samples, LAT, N_TILE, LON_DEV, D).transpose(0, 2, 1, 3, 4)
    float_grid = tok_grid.astype(jnp.float32)
    inverse = lax.rsqrt(lax.optimization_barrier(jnp.mean(float_grid * float_grid, axis=-1, keepdims=True)) + EPS)
    normed = (float_grid * inverse).astype(jnp.bfloat16)
    normed_rows = normed.reshape(-1, D)
    projected = jnp.dot(normed_rows, w_qkv, preferred_element_type=jnp.float32).astype(jnp.bfloat16)
    projected = projected.reshape(samples, N_TILE, LAT, LON_DEV, 3 * HD)
    queries = projected[..., :HD].reshape(samples, N_TILE, LAT * LON_DEV, HD)
    key_value = projected[..., HD:]
    left_band = jnp.roll(key_value[:, :, :, LON_DEV - HALO:], 1, axis=1)
    right_band = jnp.roll(key_value[:, :, :, :HALO], -1, axis=1)
    extended = jnp.concatenate([left_band, key_value, right_band], axis=3)
    extended = extended.reshape(samples, N_TILE, LAT * ext_cols, 2 * HD)
    key_part = extended[..., :HD]
    values = extended[..., HD:]
    columns = jnp.arange(ext_cols)
    left_ok = (columns < HALO)[None, :] & ((HALO - columns)[None, :] <= band[:, 0:1])
    right_ok = (columns >= LON_DEV + HALO)[None, :] & ((columns - LON_DEV - HALO + 1)[None, :] <= band[:, 1:2])
    middle = ((columns >= HALO) & (columns < LON_DEV + HALO))[None, :]
    usable = jnp.tile(middle | left_ok | right_ok, (1, LAT))
    score_scale = HD ** (-0.5)
    scores = jnp.einsum('stqh,stkh->stqk', queries.astype(jnp.float32), key_part.astype(jnp.float32)) * score_scale
    scores = jnp.where(usable[None, :, None, :], scores, -jnp.inf)
    row_max = lax.optimization_barrier(jnp.max(scores, axis=-1, keepdims=True))
    exp_scores = jnp.exp(scores - row_max)
    probs_full = exp_scores / lax.optimization_barrier(jnp.sum(exp_scores, axis=-1, keepdims=True))
    probs_low = probs_full.astype(jnp.bfloat16)
    attended = jnp.einsum('stqk,stkh->stqh', probs_low.astype(jnp.float32), values.astype(jnp.float32)).astype(jnp.bfloat16)
    grad_rows = grad_grid.reshape(-1, D)
    d_att = jnp.dot(grad_rows, w_out.T, preferred_element_type=jnp.float32).astype(jnp.bfloat16)
    d_att = d_att.reshape(samples, N_TILE, LAT * LON_DEV, HD)
    d_probs = jnp.einsum('stqh,stkh->stqk', d_att.astype(jnp.float32), values.astype(jnp.float32))
    row_inner = lax.optimization_barrier(jnp.sum(probs_full * d_probs, axis=-1, keepdims=True))
    d_scores = (probs_full * (d_probs - row_inner) * score_scale).astype(jnp.bfloat16)
    d_query = jnp.einsum('stqk,stkh->stqh', d_scores.astype(jnp.float32), key_part.astype(jnp.float32))
    d_keys = jnp.einsum('stqk,stqh->stkh', d_scores.astype(jnp.float32), queries.astype(jnp.float32))
    d_values = jnp.einsum('stqk,stqh->stkh', probs_low.astype(jnp.float32), d_att.astype(jnp.float32))
    d_ext = jnp.concatenate([d_keys, d_values], axis=-1).reshape(samples, N_TILE, LAT, ext_cols, 2 * HD)
    own_grads = d_ext[:, :, :, HALO:HALO + LON_DEV]
    from_left = jnp.roll(d_ext[:, :, :, LON_DEV + HALO:], 1, axis=1)
    from_right = jnp.roll(d_ext[:, :, :, :HALO], -1, axis=1)
    own_grads = own_grads.at[:, :, :, :HALO].add(from_left)
    own_grads = own_grads.at[:, :, :, LON_DEV - HALO:].add(from_right)
    d_qkv = jnp.concatenate([d_query.reshape(samples, N_TILE, LAT, LON_DEV, HD), own_grads], axis=-1).astype(jnp.bfloat16)
    d_normed = jnp.dot(d_qkv.reshape(-1, 3 * HD), w_qkv.T, preferred_element_type=jnp.float32).reshape(float_grid.shape)
    d_float = inverse * d_normed - float_grid * inverse ** 3 * lax.optimization_barrier(jnp.mean(d_normed * float_grid, axis=-1, keepdims=True))
    d_tokens = d_float.astype(jnp.bfloat16).transpose(0, 2, 1, 3, 4).reshape(tokens.shape)
    normed_t = jnp.swapaxes(normed.reshape(samples, N_TILE, -1, D), 0, 1)
    dqkv_t = jnp.swapaxes(d_qkv.reshape(samples, N_TILE, -1, 3 * HD), 0, 1)
    grad_t = jnp.swapaxes(grad_grid.reshape(samples, N_TILE, -1, D), 0, 1)
    att_t = jnp.swapaxes(attended.reshape(samples, N_TILE, -1, HD), 0, 1)

    def one_tile(running, slices):
        normed_s, dqkv_s, grad_s, att_s = slices
        part_qkv = jnp.einsum('sqd,sqe->sde', normed_s.astype(jnp.float32), dqkv_s.astype(jnp.float32)).astype(jnp.bfloat16)
        part_out = jnp.einsum('sqh,sqd->shd', att_s.astype(jnp.float32), grad_s.astype(jnp.float32)).astype(jnp.bfloat16)
        part_qkv, part_out = lax.optimization_barrier((part_qkv, part_out))
        total_qkv = running[0] + lax.optimization_barrier(jnp.sum(part_qkv.astype(jnp.float32), axis=0))
        total_out = running[1] + lax.optimization_barrier(jnp.sum(part_out.astype(jnp.float32), axis=0))
        return ((total_qkv, total_out), None)
    start_sums = (jnp.zeros((D, 3 * HD), jnp.float32), jnp.zeros((HD, D), jnp.float32))
    (grad_qkv, grad_out), unused = lax.scan(one_tile, start_sums, (normed_t, dqkv_t, grad_t, att_t))
    return (d_tokens, grad_qkv, grad_out)
```

```python
import jax
import jax.numpy as jnp
from jax import lax
from jax.sharding import PartitionSpec as P

HALO = 2
EPS = 1e-05
TILE = ("x", "zlo")
FSDP = ("y", "zhi", "core")
GROUPS = 4


def shift_pairs(count, step):
    return [(i, (i + step) % count) for i in range(count)]


def rms_inverse(rows):
    return lax.rsqrt(jnp.mean(rows * rows, axis=-1, keepdims=True) + EPS)


def gather_weights(w_qkv, w_out):
    x = lax.axis_index("x")
    core = lax.axis_index("core")
    head_dim = w_out.shape[0]
    block = jnp.concatenate([w_qkv, w_out.T], axis=1)
    mine = lax.dynamic_slice_in_dim(block, x * head_dim, head_dim, axis=1)
    spread = lax.all_to_all(
        jnp.broadcast_to(mine[None], (16,) + mine.shape), ("y", "zhi"), 0, 0
    )
    parts = [spread] + [
        lax.ppermute(spread, "x", shift_pairs(GROUPS, step)) for step in range(1, GROUPS)
    ]
    others = [lax.ppermute(part, "core", shift_pairs(2, 1)) for part in parts]
    order = (x - jnp.arange(GROUPS)) % GROUPS
    own = jnp.take(jnp.stack(parts), order, axis=0)
    other = jnp.take(jnp.stack(others), order, axis=0)
    both = jnp.stack([jnp.where(core == 0, own, other), jnp.where(core == 0, other, own)])
    return both.transpose(2, 0, 3, 1, 4).reshape(-1, GROUPS * head_dim)


def reduce_grads(grads):
    x = lax.axis_index("x")
    width = grads.shape[1] // GROUPS
    ordered = grads.reshape(16, 2, 128, GROUPS, width).transpose(1, 3, 0, 2, 4)
    pair = lax.all_to_all(ordered, "core", 0, 0)
    chip = (pair[0].astype(jnp.float32) + pair[1].astype(jnp.float32)).astype(jnp.bfloat16)
    total = lax.dynamic_index_in_dim(chip, x, 0, keepdims=False).astype(jnp.float32)
    for step in range(1, GROUPS):
        away = lax.dynamic_index_in_dim(chip, (x + step) % GROUPS, 0, keepdims=False)
        total = total + lax.ppermute(away, "x", shift_pairs(GROUPS, step)).astype(jnp.float32)
    line = total.astype(jnp.bfloat16).reshape(64, 32, width)
    pieces = lax.all_to_all(line, ("y", "zhi", "zlo"), 0, 0)
    piece = jnp.sum(pieces.astype(jnp.float32), axis=0).astype(jnp.bfloat16)
    full = lax.all_to_all(
        jnp.broadcast_to(piece[None], (16,) + piece.shape), TILE, 0, 0
    )
    return full.reshape(GROUPS, 128, width).astype(jnp.float32)


def local(tokens, w_qkv, w_out, band, cotangent):
    samples, lat_rows, lon_cols, features = tokens.shape
    head_dim = w_out.shape[0]
    num_rows = lat_rows * lon_cols
    edge = lat_rows * HALO
    forward = shift_pairs(16, 1)
    backward = shift_pairs(16, -1)
    low = lax.ppermute(tokens[0, :, lon_cols - HALO :], TILE, forward)
    high = lax.ppermute(tokens[0, :, :HALO], TILE, backward)
    weights = gather_weights(w_qkv, w_out)
    rows = jnp.concatenate(
        [
            tokens.reshape(num_rows, features),
            low.reshape(edge, features),
            high.reshape(edge, features),
        ],
        axis=0,
    )
    grad_rows = cotangent.reshape(num_rows, features)
    float_rows = rows.astype(jnp.float32)
    inverse = rms_inverse(float_rows)
    normed = (float_rows * inverse).astype(jnp.bfloat16)
    w_in = weights[:, : 3 * head_dim]
    w_back = weights[:, 3 * head_dim :]
    projected = jnp.dot(normed, w_in, preferred_element_type=jnp.float32).astype(jnp.bfloat16)
    queries = projected[:num_rows, :head_dim]
    keys = projected[:, head_dim : 2 * head_dim]
    values = projected[:, 2 * head_dim :]
    place = jnp.arange(num_rows + 2 * edge)
    column = (place - num_rows) % HALO
    usable = (
        (place < num_rows)
        | ((place < num_rows + edge) & (HALO - column <= band[0, 0]))
        | ((place >= num_rows + edge) & (column + 1 <= band[0, 1]))
    )
    score_scale = head_dim ** (-0.5)
    scores = (
        lax.dot_general(
            queries, keys, (((1,), (1,)), ((), ())), preferred_element_type=jnp.float32
        )
        * score_scale
    )
    scores = jnp.where(usable[None, :], scores, -jnp.inf)
    exp_scores = jnp.exp(scores - jnp.max(scores, axis=-1, keepdims=True))
    probs_full = exp_scores / jnp.sum(exp_scores, axis=-1, keepdims=True)
    probs_low = probs_full.astype(jnp.bfloat16)
    attended = jnp.dot(probs_low, values, preferred_element_type=jnp.float32).astype(jnp.bfloat16)
    d_att = jnp.dot(grad_rows, w_back, preferred_element_type=jnp.float32).astype(jnp.bfloat16)
    d_probs = lax.dot_general(
        d_att, values, (((1,), (1,)), ((), ())), preferred_element_type=jnp.float32
    )
    row_inner = jnp.sum(probs_full * d_probs, axis=-1, keepdims=True)
    d_scores = (probs_full * (d_probs - row_inner) * score_scale).astype(jnp.bfloat16)
    d_query = jnp.dot(d_scores, keys, preferred_element_type=jnp.float32)
    over_rows = (((0,), (0,)), ((), ()))
    d_keys = lax.dot_general(d_scores, queries, over_rows, preferred_element_type=jnp.float32)
    d_values = lax.dot_general(probs_low, d_att, over_rows, preferred_element_type=jnp.float32)
    d_kv = jnp.concatenate([d_keys, d_values], axis=1)
    edges = d_kv[num_rows:].astype(jnp.bfloat16)
    to_left = lax.ppermute(edges[:edge], TILE, backward)
    to_right = lax.ppermute(edges[edge:], TILE, forward)
    d_ext = jnp.concatenate(
        [jnp.pad(d_query, ((0, 2 * edge), (0, 0))), d_kv], axis=1
    ).astype(jnp.bfloat16)
    first_term = lax.dot_general(normed, d_ext, over_rows, preferred_element_type=jnp.float32)
    second_term = lax.dot_general(
        grad_rows, attended, over_rows, preferred_element_type=jnp.float32
    )
    grads = reduce_grads(jnp.concatenate([first_term, second_term], axis=1).astype(jnp.bfloat16))
    own = d_kv[:num_rows].reshape(lat_rows, lon_cols, 2 * head_dim)
    own = own.at[:, lon_cols - HALO :].add(
        to_left.astype(jnp.float32).reshape(lat_rows, HALO, 2 * head_dim)
    )
    own = own.at[:, :HALO].add(
        to_right.astype(jnp.float32).reshape(lat_rows, HALO, 2 * head_dim)
    )
    d_qkv = jnp.concatenate([d_query, own.reshape(num_rows, 2 * head_dim)], axis=1).astype(
        jnp.bfloat16
    )
    d_normed = lax.dot_general(
        d_qkv, w_in, (((1,), (1,)), ((), ())), preferred_element_type=jnp.float32
    )
    own_inverse = inverse[:num_rows]
    own_rows = float_rows[:num_rows]
    d_float = own_inverse * d_normed - own_rows * own_inverse**3 * jnp.mean(
        d_normed * own_rows, axis=-1, keepdims=True
    )
    d_tokens = d_float.astype(jnp.bfloat16).reshape(tokens.shape)
    grad_qkv = jnp.concatenate([grads[0], grads[1], grads[2]], axis=1)
    return (d_tokens, grad_qkv, grads[3].T)


def solution(mesh):
    inner = jax.sharding.Mesh(
        mesh.devices.reshape(4, 4, 8, 2, 2), ("x", "zlo", "y", "zhi", "core")
    )
    placed = (
        P(FSDP, None, TILE, None),
        P(FSDP, None),
        P(None, FSDP),
        P(TILE, None),
        P(FSDP, None, TILE, None),
    )
    return jax.shard_map(
        local,
        mesh=inner,
        in_specs=placed,
        out_specs=(P(FSDP, None, TILE, None), P(FSDP, None), P(None, FSDP)),
        check_vma=False,
    )
```

```python
import functools

import jax
import jax.numpy as jnp
from jax import lax
from jax.experimental import pallas as pl
from jax.experimental.pallas import tpu as pltpu
from jax.sharding import PartitionSpec as P

HALO = 2
EPS = 1e-05
TILE = ("x", "zlo")
FSDP = ("y", "zhi", "core")
GROUPS = 4
HD = 128
ROWS = 192
EDGE = 24
EXT = ROWS + 2 * EDGE
BLOCKS = 16
CHUNK = 4
VMEM_BYTES = 40 * 1024 * 1024
OVER_ROWS = (((0,), (0,)), ((), ()))
OVER_COLS = (((1,), (1,)), ((), ()))
F32 = jnp.float32
BF16 = jnp.bfloat16


def shift_pairs(count, step):
    return [(i, (i + step) % count) for i in range(count)]


def dot(a, b, dims=(((1,), (0,)), ((), ()))):
    return lax.dot_general(a, b, dims, preferred_element_type=F32)


def feature_block(block, core):
    return pl.ds(pl.multiple_of((2 * block + core) * HD, HD), HD)


def features_of(ref, first, core):
    return jnp.concatenate(
        [ref[:, feature_block(block, core)] for block in range(first, first + CHUNK)], axis=1
    )


def project(rows_ref, own_ref, other_ref, core):
    total = jnp.zeros((rows_ref.shape[0], HD), F32)
    for part, side in ((own_ref, core), (other_ref, 1 - core)):
        for first in range(0, BLOCKS, CHUNK):
            weights = part[first : first + CHUNK].reshape(CHUNK * HD, HD)
            total = total + dot(features_of(rows_ref, first, side), weights)
    return total.astype(BF16)


def store_grads(out_ref, left_qkv, left_out, normed_ref, cot_ref, x, side):
    for first in range(0, BLOCKS, CHUNK):
        qkv = dot(left_qkv, features_of(normed_ref, first, side)).astype(BF16)
        out = dot(left_out, features_of(cot_ref, first, side)).astype(BF16)
        for group in range(GROUPS):
            slot = (group - x + GROUPS) % GROUPS
            for block in range(CHUNK):
                columns = slice(block * HD, (block + 1) * HD)
                if group < 3:
                    value = qkv[group * HD : (group + 1) * HD, columns]
                else:
                    value = out[:, columns]
                out_ref[slot, first + block] = value


def attention_kernel(
    place_ref, band_ref, normed_ref, cot_ref, *refs
):
    own = refs[:GROUPS]
    other = refs[GROUPS : 2 * GROUPS]
    away_ref, left_qkv_ref, left_out_ref, own_grads_ref, edges_ref, proj, datt = refs[2 * GROUPS :]
    x = place_ref[0]
    core = place_ref[1]
    for step in range(GROUPS):
        group = (x - step + GROUPS) % GROUPS

        @pl.when(group == 3)
        def _():
            datt[...] = project(cot_ref, own[step], other[step], core)

        @pl.when(group != 3)
        def _():
            proj[group] = project(normed_ref, own[step], other[step], core)

    queries = proj[0][:ROWS]
    keys = proj[1]
    values = proj[2]
    d_att = datt[...]
    place = lax.broadcasted_iota(jnp.int32, (1, EXT), 1)
    column = (place - ROWS) % HALO
    usable = (
        (place < ROWS)
        | ((place < ROWS + EDGE) & (HALO - column <= band_ref[0, 0]))
        | ((place >= ROWS + EDGE) & (column + 1 <= band_ref[0, 1]))
    )
    scale = HD ** (-0.5)
    scores = jnp.where(usable, dot(queries, keys, OVER_COLS) * scale, -jnp.inf)
    exp_scores = jnp.exp(scores - jnp.max(scores, axis=-1, keepdims=True))
    probs = exp_scores / jnp.sum(exp_scores, axis=-1, keepdims=True)
    probs_low = probs.astype(BF16)
    attended = dot(probs_low, values).astype(BF16)
    d_probs = dot(d_att, values, OVER_COLS)
    inner = jnp.sum(probs * d_probs, axis=-1, keepdims=True)
    d_scores = (probs * (d_probs - inner) * scale).astype(BF16)
    d_query = dot(d_scores, keys)
    d_keys = dot(d_scores, queries, OVER_ROWS)
    d_values = dot(probs_low, d_att, OVER_ROWS)
    own_grads_ref[:, :HD] = d_query
    own_grads_ref[:, HD : 2 * HD] = d_keys[:ROWS]
    own_grads_ref[:, 2 * HD :] = d_values[:ROWS]
    edges_ref[:, :HD] = d_keys[ROWS:].astype(BF16)
    edges_ref[:, HD:] = d_values[ROWS:].astype(BF16)
    d_query_ext = jnp.concatenate([d_query, jnp.zeros((2 * EDGE, HD), F32)], axis=0)
    left_qkv = jnp.concatenate([d_query_ext.T, d_keys.T, d_values.T], axis=0).astype(BF16)
    left_out = attended.astype(F32).T.astype(BF16)
    left_qkv_ref[...] = left_qkv
    left_out_ref[...] = left_out
    store_grads(away_ref, left_qkv, left_out, normed_ref, cot_ref, x, 1 - core)


def own_half_kernel(place_ref, left_qkv_ref, left_out_ref, normed_ref, cot_ref, out_ref):
    store_grads(
        out_ref,
        left_qkv_ref[...],
        left_out_ref[...],
        normed_ref,
        cot_ref,
        place_ref[0],
        place_ref[1],
    )


def tokens_kernel(place_ref, d_qkv_ref, tokens_ref, inverse_ref, *refs):
    own = refs[:GROUPS]
    other = refs[GROUPS : 2 * GROUPS]
    out_ref, d_normed = refs[2 * GROUPS :]
    x = place_ref[0]
    core = place_ref[1]
    left = jnp.concatenate(
        [d_qkv_ref[(x - step + GROUPS) % GROUPS] for step in range(GROUPS)], axis=1
    )
    total = jnp.zeros((ROWS, HD), F32)
    for parts, side in ((own, core), (other, 1 - core)):
        for block in range(BLOCKS):
            weights = jnp.concatenate([part[block] for part in parts], axis=1)
            piece = dot(left, weights, OVER_COLS)
            columns = feature_block(block, side)
            d_normed[:, columns] = piece
            total = total + piece * tokens_ref[:, columns].astype(F32)
    inverse = inverse_ref[...]
    mean = jnp.sum(total, axis=-1, keepdims=True) * (1.0 / (2 * BLOCKS * HD))
    factor = inverse * inverse * inverse * mean
    for block in range(2 * BLOCKS):
        columns = slice(block * HD, (block + 1) * HD)
        out_ref[:, columns] = (
            inverse * d_normed[:, columns] - tokens_ref[:, columns].astype(F32) * factor
        ).astype(BF16)


def call(body, operands, outs, scratch, flops, in_bytes, smem):
    whole = pl.BlockSpec(memory_space=pltpu.VMEM)
    scalars = pl.BlockSpec(memory_space=pltpu.SMEM)
    return pl.pallas_call(
        body,
        in_specs=[scalars] * smem + [whole] * (len(operands) - smem),
        out_specs=[whole] * len(outs),
        out_shape=[jax.ShapeDtypeStruct(shape, dtype) for shape, dtype in outs],
        scratch_shapes=[pltpu.VMEM(shape, dtype) for shape, dtype in scratch],
        compiler_params=pltpu.CompilerParams(vmem_limit_bytes=VMEM_BYTES),
        cost_estimate=pl.CostEstimate(
            flops=flops, bytes_accessed=in_bytes, transcendentals=0
        ),
    )(*operands)


def gather_weights(w_qkv, w_out, x):
    block = jnp.concatenate([w_qkv, w_out.T], axis=1)
    mine = lax.dynamic_slice_in_dim(block, x * HD, HD, axis=1)
    spread = lax.all_to_all(
        jnp.broadcast_to(mine[None], (BLOCKS,) + mine.shape), ("y", "zhi"), 0, 0
    )
    own = [spread] + [
        lax.ppermute(spread, "x", shift_pairs(GROUPS, step)) for step in range(1, GROUPS)
    ]
    other = [lax.ppermute(part, "core", shift_pairs(2, 1)) for part in own]
    return own, other


def local(tokens, w_qkv, w_out, band, cotangent):
    samples, lat_rows, lon_cols, features = tokens.shape
    x = lax.axis_index("x")
    core = lax.axis_index("core")
    place = jnp.stack([x, core]).astype(jnp.int32)
    forward = shift_pairs(16, 1)
    backward = shift_pairs(16, -1)
    own, other = gather_weights(w_qkv, w_out, x)
    tok_rows = tokens.reshape(ROWS, features)
    cot_rows = cotangent.reshape(ROWS, features)
    halo_in, unused = lax.optimization_barrier((tokens[0], own[0]))
    low = lax.ppermute(halo_in[:, lon_cols - HALO :], TILE, forward)
    high = lax.ppermute(halo_in[:, :HALO], TILE, backward)

    def normalise(rows):
        rows = rows.astype(F32)
        inverse = lax.rsqrt(jnp.mean(rows * rows, axis=-1, keepdims=True) + EPS)
        return (rows * inverse).astype(BF16), inverse

    normed_own, inverse = normalise(tok_rows)
    normed_low, unused = normalise(low.reshape(EDGE, features))
    normed_high, unused = normalise(high.reshape(EDGE, features))
    normed = jnp.concatenate([normed_own, normed_low, normed_high], axis=0)

    grad_shape = ((GROUPS, BLOCKS, HD, HD), BF16)
    away, left_qkv, left_out, own_grads, edges = call(
        attention_kernel,
        [place, band, normed, cot_rows, *own, *other],
        [
            grad_shape,
            ((3 * HD, EXT), BF16),
            ((HD, ROWS), BF16),
            ((ROWS, 3 * HD), F32),
            ((2 * EDGE, 2 * HD), BF16),
        ],
        [((3, EXT, HD), BF16), ((ROWS, HD), BF16)],
        3_000_000_000,
        12_000_000,
        2,
    )
    received = lax.ppermute(away, "core", shift_pairs(2, 1))
    (kept,) = call(
        own_half_kernel,
        [place, left_qkv, left_out, normed, cot_rows],
        [grad_shape],
        [],
        500_000_000,
        6_000_000,
        1,
    )
    chip = [
        (kept[step].astype(F32) + received[step].astype(F32)).astype(BF16)
        for step in range(GROUPS)
    ]
    total = chip[0].astype(F32)
    for step in range(1, GROUPS):
        total = total + lax.ppermute(chip[step], "x", shift_pairs(GROUPS, step)).astype(F32)
    line = total.astype(BF16)
    line, edges = lax.optimization_barrier((line, edges))
    pieces = lax.all_to_all(line.reshape(64, 32, HD), ("y", "zhi", "zlo"), 0, 0)
    piece = jnp.sum(pieces.astype(F32), axis=0).astype(BF16)
    full = lax.all_to_all(jnp.broadcast_to(piece[None], (16,) + piece.shape), TILE, 0, 0)
    grads = full.reshape(GROUPS * HD, HD).astype(F32)

    to_left = lax.ppermute(edges[:EDGE], TILE, backward)
    to_right = lax.ppermute(edges[EDGE:], TILE, forward)
    d_kv = own_grads[:, HD:].reshape(lat_rows, lon_cols, 2 * HD)
    d_kv = d_kv.at[:, lon_cols - HALO :].add(
        to_left.astype(F32).reshape(lat_rows, HALO, 2 * HD)
    )
    d_kv = d_kv.at[:, :HALO].add(to_right.astype(F32).reshape(lat_rows, HALO, 2 * HD))
    d_kv = d_kv.reshape(ROWS, 2 * HD)
    d_qkv = jnp.stack(
        [own_grads[:, :HD], d_kv[:, :HD], d_kv[:, HD:], jnp.zeros((ROWS, HD), F32)]
    ).astype(BF16)
    (d_tokens,) = call(
        tokens_kernel,
        [place, d_qkv, tok_rows, inverse, *own, *other],
        [((ROWS, features), BF16)],
        [((ROWS, features), F32)],
        800_000_000,
        8_000_000,
        1,
    )
    return (d_tokens.reshape(tokens.shape), grads[: 3 * HD].T, grads[3 * HD :])


def solution(mesh):
    inner = jax.sharding.Mesh(
        mesh.devices.reshape(4, 4, 8, 2, 2), ("x", "zlo", "y", "zhi", "core")
    )
    placed = (
        P(FSDP, None, TILE, None),
        P(FSDP, None),
        P(None, FSDP),
        P(TILE, None),
        P(FSDP, None, TILE, None),
    )
    return jax.shard_map(
        local,
        mesh=inner,
        in_specs=placed,
        out_specs=(P(FSDP, None, TILE, None), P(FSDP, None), P(None, FSDP)),
        check_vma=False,
    )
```

```python
import functools

import jax
import jax.numpy as jnp
from jax import lax
from jax.experimental import pallas as pl
from jax.experimental.pallas import tpu as pltpu
from jax.sharding import PartitionSpec as P

HALO = 2
EPS = 1e-05
TILE = ("x", "zlo")
FSDP = ("y", "zhi", "core")
GROUPS = 4
HD = 128
ROWS = 192
EDGE = 24
PAD = 32
EXT = ROWS + 2 * PAD
STEPS = (2, 1, 3)
BLOCKS = 16
CHUNK = 4
VMEM_BYTES = 40 * 1024 * 1024
OVER_ROWS = (((0,), (0,)), ((), ()))
OVER_COLS = (((1,), (1,)), ((), ()))
F32 = jnp.float32
BF16 = jnp.bfloat16


def shift_pairs(count, step):
    return [(i, (i + step) % count) for i in range(count)]


def dot(a, b, dims=(((1,), (0,)), ((), ()))):
    return lax.dot_general(a, b, dims, preferred_element_type=F32)


def feature_block(block, core):
    return pl.ds(pl.multiple_of((2 * block + core) * HD, HD), HD)


def features_of(refs, first, core):
    columns = [
        jnp.concatenate([ref[:, feature_block(block, core)] for ref in refs], axis=0)
        for block in range(first, first + CHUNK)
    ]
    return jnp.concatenate(columns, axis=1)


def edge_chooser(shape, row_axis):
    row = lax.broadcasted_iota(jnp.int32, shape, row_axis)
    edge = lax.broadcasted_iota(jnp.int32, shape, 1 - row_axis)
    column = row % 16
    base = (row // 16) * HALO
    last = (column >= 16 - HALO) & (edge == base + column - (16 - HALO))
    first = (column < HALO) & (edge == base + column)
    return first, last


def as_weights(mask):
    return jnp.where(mask, 1.0, 0.0).astype(BF16)


def normalise_kernel(tokens_ref, normed_ref, inverse_ref, first_ref, last_ref):
    total = jnp.zeros((ROWS, HD), F32)
    for block in range(2 * BLOCKS):
        piece = tokens_ref[:, block * HD : (block + 1) * HD].astype(F32)
        total = total + piece * piece
    mean = jnp.sum(total, axis=-1, keepdims=True) * (1.0 / (2 * BLOCKS * HD))
    inverse = lax.rsqrt(mean + EPS)
    inverse_ref[...] = inverse
    first, last = edge_chooser((PAD, ROWS), 1)
    first, last = as_weights(first), as_weights(last)
    for block in range(0, 2 * BLOCKS, CHUNK):
        columns = slice(block * HD, (block + CHUNK) * HD)
        piece = (tokens_ref[:, columns].astype(F32) * inverse).astype(BF16)
        normed_ref[:, columns] = piece
        first_ref[:, columns] = dot(first, piece).astype(BF16)
        last_ref[:, columns] = dot(last, piece).astype(BF16)


def project(rows_refs, parts, core):
    total = None
    for part, side in zip(parts, (core, 1 - core)):
        for first in range(0, BLOCKS, CHUNK):
            term = dot(features_of(rows_refs, first, side), part(first))
            total = term if total is None else total + term
    return total.astype(BF16)


def columns_of(refs):
    def weights(first):
        return jnp.concatenate(
            [ref[first : first + CHUNK].reshape(CHUNK * HD, HD) for ref in refs], axis=1
        )

    return weights


def pick(values, index):
    chosen = values[0]
    for place in range(1, len(values)):
        chosen = jnp.where(index == place, values[place], chosen)
    return chosen


def project_back(rows_refs, parts, core):
    total = None
    for ref, side in zip(parts, (core, 1 - core)):
        for first in range(0, BLOCKS, CHUNK):
            blocks = [ref[block] for block in range(first, first + CHUNK)]
            term = dot(
                features_of(rows_refs, first, side), jnp.concatenate(blocks, axis=1), OVER_COLS
            )
            total = term if total is None else total + term
    return total.astype(BF16)


def store_grads(first_ref, rest_ref, left_qkv, left_out, normed_refs, cot_ref, x, side):
    for first in range(0, BLOCKS, CHUNK):
        qkv = dot(left_qkv, features_of(normed_refs, first, side)).astype(BF16)
        out = dot(left_out, features_of([cot_ref], first, side)).astype(BF16)
        groups = [qkv[:HD], qkv[HD : 2 * HD], qkv[2 * HD :], out]
        for block in range(CHUNK):
            columns = slice(block * HD, (block + 1) * HD)
            values = [value[:, columns] for value in groups]
            first_ref[first + block] = pick(values, x)
            for step in range(1, GROUPS):
                rest_ref[step - 1, first + block] = pick(values[step:] + values[:step], x)


def attention_kernel(place_ref, band_ref, normed_ref, low_ref, high_ref, cot_ref, *refs):
    own, other = refs[:GROUPS], refs[GROUPS : 2 * GROUPS]
    (
        away_first_ref,
        away_rest_ref,
        left_qkv_ref,
        left_out_ref,
        own_grads_ref,
        low_back_ref,
        high_back_ref,
        proj,
        datt,
    ) = refs[2 * GROUPS :]
    x = place_ref[0]
    core = place_ref[1]
    normed_refs = [normed_ref, low_ref, high_ref]

    for position in range(GROUPS):
        steps = [(position - group) % GROUPS for group in range(GROUPS)]

        @pl.when(x == position)
        def _():
            proj[...] = project(
                normed_refs,
                (
                    columns_of([own[step] for step in steps[:3]]),
                    columns_of([other[step] for step in steps[:3]]),
                ),
                core,
            )
            datt[...] = project_back([cot_ref], (own[steps[3]], other[steps[3]]), core)

    queries = proj[:ROWS, :HD]
    keys = proj[:, HD : 2 * HD]
    values = proj[:, 2 * HD :]
    d_att = datt[...]
    place = lax.broadcasted_iota(jnp.int32, (1, EXT), 1)
    column = (place - ROWS) % HALO
    low = (place >= ROWS) & (place < ROWS + EDGE)
    high = (place >= ROWS + PAD) & (place < ROWS + PAD + EDGE)
    usable = (
        (place < ROWS)
        | (low & (HALO - column <= band_ref[0, 0]))
        | (high & (column + 1 <= band_ref[0, 1]))
    )
    scale = HD ** (-0.5)
    scores = jnp.where(usable, dot(queries, keys, OVER_COLS) * scale, -jnp.inf)
    exp_scores = jnp.exp(scores - jnp.max(scores, axis=-1, keepdims=True))
    probs = exp_scores / jnp.sum(exp_scores, axis=-1, keepdims=True)
    probs_low = probs.astype(BF16)
    attended = dot(probs_low, values).astype(BF16)
    d_probs = dot(d_att, values, OVER_COLS)
    inner = jnp.sum(probs * d_probs, axis=-1, keepdims=True)
    d_scores = (probs * (d_probs - inner) * scale).astype(BF16)
    d_query = dot(d_scores, keys)
    d_keys = dot(d_scores, queries, OVER_ROWS)
    d_values = dot(probs_low, d_att, OVER_ROWS)
    own_grads_ref[:, :HD] = d_query
    own_grads_ref[:, HD : 2 * HD] = d_keys[:ROWS]
    own_grads_ref[:, 2 * HD :] = d_values[:ROWS]
    for ref, start in ((low_back_ref, ROWS), (high_back_ref, ROWS + PAD)):
        ref[:, :HD] = d_keys[start : start + PAD].astype(BF16)
        ref[:, HD:] = d_values[start : start + PAD].astype(BF16)
    d_query_ext = jnp.concatenate([d_query, jnp.zeros((2 * PAD, HD), F32)], axis=0)
    left_qkv = jnp.concatenate([d_query_ext.T, d_keys.T, d_values.T], axis=0).astype(BF16)
    left_out = attended.astype(F32).T.astype(BF16)
    left_qkv_ref[...] = left_qkv
    left_out_ref[...] = left_out
    store_grads(
        away_first_ref, away_rest_ref, left_qkv, left_out, normed_refs, cot_ref, x, 1 - core
    )


def own_half_kernel(place_ref, left_qkv_ref, left_out_ref, *refs):
    normed_refs, cot_ref, first_ref, rest_ref = refs[:3], refs[3], refs[4], refs[5]
    store_grads(
        first_ref,
        rest_ref,
        left_qkv_ref[...],
        left_out_ref[...],
        normed_refs,
        cot_ref,
        place_ref[0],
        place_ref[1],
    )


def spread_kernel(place_ref, w_qkv_ref, w_out_ref, out_ref):
    columns = [w_qkv_ref[:, group * HD : (group + 1) * HD] for group in range(3)]
    mine = pick(columns + [w_out_ref[...]], place_ref[0])
    for block in range(BLOCKS):
        out_ref[block] = mine


def piece_kernel(pieces_ref, out_ref):
    total = pieces_ref[0].astype(F32)
    for source in range(1, pieces_ref.shape[0]):
        total = total + pieces_ref[source].astype(F32)
    total = total.astype(BF16)
    for target in range(out_ref.shape[0]):
        out_ref[target] = total


def final_kernel(full_ref, qkv_ref, out_ref):
    for group in range(GROUPS):
        value = jnp.concatenate(
            [full_ref[4 * group + quarter].astype(F32) for quarter in range(4)], axis=0
        )
        if group < 3:
            qkv_ref[:, group * HD : (group + 1) * HD] = value.T
        else:
            out_ref[...] = value


def line_kernel(*refs):
    for block in range(BLOCKS):
        total = refs[0][block].astype(F32)
        for ref in refs[1:-1]:
            total = total + ref[block].astype(F32)
        refs[-1][block] = total.astype(BF16)


def tokens_kernel(
    place_ref, grads_ref, from_left_ref, from_right_ref, tokens_ref, inverse_ref, *refs
):
    own, other = refs[:GROUPS], refs[GROUPS : 2 * GROUPS]
    out_ref, d_normed, d_qkv = refs[2 * GROUPS :]
    x = place_ref[0]
    core = place_ref[1]
    first, last = edge_chooser((ROWS, PAD), 0)
    d_kv = (
        grads_ref[:, HD:]
        + dot(as_weights(first), from_left_ref[...])
        + dot(as_weights(last), from_right_ref[...])
    )
    d_qkv[0] = grads_ref[:, :HD].astype(BF16)
    d_qkv[1] = d_kv[:, :HD].astype(BF16)
    d_qkv[2] = d_kv[:, HD:].astype(BF16)
    d_qkv[3] = jnp.zeros((ROWS, HD), BF16)
    left = jnp.concatenate(
        [d_qkv[(x - step + GROUPS) % GROUPS] for step in range(GROUPS)], axis=1
    )
    total = jnp.zeros((ROWS, HD), F32)
    for parts, side in ((own, core), (other, 1 - core)):
        for block in range(BLOCKS):
            weights = jnp.concatenate([part[block] for part in parts], axis=1)
            piece = dot(left, weights, OVER_COLS)
            columns = feature_block(block, side)
            d_normed[:, columns] = piece
            total = total + piece * tokens_ref[:, columns].astype(F32)
    inverse = inverse_ref[...]
    mean = jnp.sum(total, axis=-1, keepdims=True) * (1.0 / (2 * BLOCKS * HD))
    factor = inverse * inverse * inverse * mean
    for block in range(2 * BLOCKS):
        columns = slice(block * HD, (block + 1) * HD)
        out_ref[:, columns] = (
            inverse * d_normed[:, columns] - tokens_ref[:, columns].astype(F32) * factor
        ).astype(BF16)


def call(body, operands, outs, scratch, flops, in_bytes, smem):
    whole = pl.BlockSpec(memory_space=pltpu.VMEM)
    scalars = pl.BlockSpec(memory_space=pltpu.SMEM)
    return pl.pallas_call(
        body,
        in_specs=[scalars] * smem + [whole] * (len(operands) - smem),
        out_specs=[whole] * len(outs),
        out_shape=[jax.ShapeDtypeStruct(shape, dtype) for shape, dtype in outs],
        scratch_shapes=[pltpu.VMEM(shape, dtype) for shape, dtype in scratch],
        compiler_params=pltpu.CompilerParams(vmem_limit_bytes=VMEM_BYTES),
        cost_estimate=pl.CostEstimate(
            flops=flops, bytes_accessed=in_bytes, transcendentals=0
        ),
    )(*operands)


def local(tokens, w_qkv, w_out, band, cotangent):
    samples, lat_rows, lon_cols, features = tokens.shape
    place = jnp.stack([lax.axis_index("x"), lax.axis_index("core")]).astype(jnp.int32)
    forward = shift_pairs(16, 1)
    backward = shift_pairs(16, -1)
    swap = shift_pairs(2, 1)
    tok_rows = tokens.reshape(ROWS, features)
    cot_rows = cotangent.reshape(ROWS, features)
    (spread,) = call(
        spread_kernel, [place, w_qkv, w_out], [((BLOCKS, HD, HD), BF16)], [], 1_000_000, 500_000, 1
    )
    spread = lax.all_to_all(spread, ("y", "zhi"), 0, 0)
    steps = {step: lax.ppermute(spread, "x", shift_pairs(GROUPS, step)) for step in STEPS}
    own = [spread, steps[1], steps[2], steps[3]]
    late_rows, unused = lax.optimization_barrier((tok_rows, spread))
    normed_own, inverse, first, last = call(
        normalise_kernel,
        [late_rows],
        [
            ((ROWS, features), BF16),
            ((ROWS, 1), F32),
            ((PAD, features), BF16),
            ((PAD, features), BF16),
        ],
        [],
        200_000_000,
        3_000_000,
        0,
    )
    low = lax.ppermute(last, TILE, forward)
    high = lax.ppermute(first, TILE, backward)
    own[3], low, high = lax.optimization_barrier((own[3], low, high))
    normed = [normed_own, low, high]
    other = [lax.ppermute(part, "core", swap) for part in own]

    first_shape = ((BLOCKS, HD, HD), BF16)
    rest_shape = ((GROUPS - 1, BLOCKS, HD, HD), BF16)
    away_first, away_rest, left_qkv, left_out, own_grads, low_back, high_back = call(
        attention_kernel,
        [place, band, *normed, cot_rows, *own, *other],
        [
            first_shape,
            rest_shape,
            ((3 * HD, EXT), BF16),
            ((HD, ROWS), BF16),
            ((ROWS, 3 * HD), F32),
            ((PAD, 2 * HD), BF16),
            ((PAD, 2 * HD), BF16),
        ],
        [((EXT, 3 * HD), BF16), ((ROWS, HD), BF16)],
        3_000_000_000,
        12_000_000,
        2,
    )
    got_rest = lax.ppermute(away_rest, "core", swap)
    got_first = lax.ppermute(away_first, "core", swap)
    kept_first, kept_rest = call(
        own_half_kernel,
        [place, left_qkv, left_out, *normed, cot_rows],
        [first_shape, rest_shape],
        [],
        500_000_000,
        6_000_000,
        1,
    )
    sent = [
        (kept_rest[step].astype(F32) + got_rest[step].astype(F32)).astype(BF16)
        for step in range(GROUPS - 1)
    ]
    sent, low_back, high_back = lax.optimization_barrier((sent, low_back, high_back))
    arrived = [
        lax.ppermute(sent[step - 1], "x", shift_pairs(GROUPS, step)) for step in STEPS
    ]
    from_right = lax.ppermute(low_back, TILE, backward)
    from_left = lax.ppermute(high_back, TILE, forward)
    (line,) = call(
        line_kernel,
        [kept_first, got_first, *arrived],
        [first_shape],
        [],
        2_000_000,
        3_000_000,
        0,
    )
    line, from_left, from_right = lax.optimization_barrier((line, from_left, from_right))
    pieces = lax.all_to_all(line.reshape(64, 32, HD), ("y", "zhi", "zlo"), 0, 0)
    (d_tokens,) = call(
        tokens_kernel,
        [place, own_grads, from_left, from_right, tok_rows, inverse, *own, *other],
        [((ROWS, features), BF16)],
        [((ROWS, features), F32), ((GROUPS, ROWS, HD), BF16)],
        800_000_000,
        8_000_000,
        1,
    )
    pieces, d_tokens = lax.optimization_barrier((pieces, d_tokens))
    (piece,) = call(
        piece_kernel, [pieces], [((16, 32, HD), BF16)], [], 1_000_000, 1_000_000, 0
    )
    full = lax.all_to_all(piece, TILE, 0, 0)
    grad_qkv, grad_out = call(
        final_kernel, [full], [((HD, 3 * HD), F32), ((HD, HD), F32)], [], 1_000_000, 500_000, 0
    )
    return (d_tokens.reshape(tokens.shape), grad_qkv, grad_out)


def solution(mesh):
    inner = jax.sharding.Mesh(
        mesh.devices.reshape(4, 4, 8, 2, 2), ("x", "zlo", "y", "zhi", "core")
    )
    placed = (
        P(FSDP, None, TILE, None),
        P(FSDP, None),
        P(None, FSDP),
        P(TILE, None),
        P(FSDP, None, TILE, None),
    )
    return jax.shard_map(
        local,
        mesh=inner,
        in_specs=placed,
        out_specs=(P(FSDP, None, TILE, None), P(FSDP, None), P(None, FSDP)),
        check_vma=False,
    )
```

```python
import functools

import jax
import jax.numpy as jnp
from jax import lax
from jax.experimental import pallas as pl
from jax.experimental.pallas import tpu as pltpu
from jax.sharding import PartitionSpec as P

HALO = 2
EPS = 1e-05
TILE = ("x", "zlo")
FSDP = ("y", "zhi", "core")
GROUPS = 4
HD = 128
ROWS = 192
EDGE = 24
PAD = 32
EXT = ROWS + 2 * PAD
STEPS = (2, 1, 3)
BLOCKS = 16
CHUNK = 4
VMEM_BYTES = 40 * 1024 * 1024
OVER_ROWS = (((0,), (0,)), ((), ()))
OVER_COLS = (((1,), (1,)), ((), ()))
F32 = jnp.float32
BF16 = jnp.bfloat16


def shift_pairs(count, step):
    return [(i, (i + step) % count) for i in range(count)]


def dot(a, b, dims=(((1,), (0,)), ((), ()))):
    return lax.dot_general(a, b, dims, preferred_element_type=F32)


def feature_block(block, core):
    zhi, y = divmod(block, 8)
    return pl.ds(pl.multiple_of((2 * (2 * y + zhi) + core) * HD, HD), HD)


def features_of(refs, first, core):
    columns = [
        jnp.concatenate([ref[:, feature_block(block, core)] for ref in refs], axis=0)
        for block in range(first, first + CHUNK)
    ]
    return jnp.concatenate(columns, axis=1)


def edge_chooser(shape, row_axis):
    row = lax.broadcasted_iota(jnp.int32, shape, row_axis)
    edge = lax.broadcasted_iota(jnp.int32, shape, 1 - row_axis)
    column = row % 16
    base = (row // 16) * HALO
    last = (column >= 16 - HALO) & (edge == base + column - (16 - HALO))
    first = (column < HALO) & (edge == base + column)
    return first, last


def as_weights(mask):
    return jnp.where(mask, 1.0, 0.0).astype(BF16)


def normalise_kernel(tokens_ref, normed_ref, inverse_ref, first_ref, last_ref):
    total = jnp.zeros((ROWS, HD), F32)
    for block in range(2 * BLOCKS):
        piece = tokens_ref[:, block * HD : (block + 1) * HD].astype(F32)
        total = total + piece * piece
    mean = jnp.sum(total, axis=-1, keepdims=True) * (1.0 / (2 * BLOCKS * HD))
    inverse = lax.rsqrt(mean + EPS)
    inverse_ref[...] = inverse
    first, last = edge_chooser((PAD, ROWS), 1)
    first, last = as_weights(first), as_weights(last)
    for block in range(0, 2 * BLOCKS, CHUNK):
        columns = slice(block * HD, (block + CHUNK) * HD)
        piece = (tokens_ref[:, columns].astype(F32) * inverse).astype(BF16)
        normed_ref[:, columns] = piece
        first_ref[:, columns] = dot(first, piece).astype(BF16)
        last_ref[:, columns] = dot(last, piece).astype(BF16)


def project(rows_refs, parts, core):
    total = None
    for part, side in zip(parts, (core, 1 - core)):
        for first in range(0, BLOCKS, CHUNK):
            term = dot(features_of(rows_refs, first, side), part(first))
            total = term if total is None else total + term
    return total.astype(BF16)


def columns_of(refs):
    def weights(first):
        return jnp.concatenate(
            [ref[first : first + CHUNK].reshape(CHUNK * HD, HD) for ref in refs], axis=1
        )

    return weights


def pick(values, index):
    chosen = values[0]
    for place in range(1, len(values)):
        chosen = jnp.where(index == place, values[place], chosen)
    return chosen


def project_back(rows_refs, parts, core):
    total = None
    for ref, side in zip(parts, (core, 1 - core)):
        for first in range(0, BLOCKS, CHUNK):
            blocks = [ref[block] for block in range(first, first + CHUNK)]
            term = dot(
                features_of(rows_refs, first, side), jnp.concatenate(blocks, axis=1), OVER_COLS
            )
            total = term if total is None else total + term
    return total.astype(BF16)


def store_grads(first_ref, rest_ref, left_qkv, left_out, normed_refs, cot_ref, x, side):
    for first in range(0, BLOCKS, CHUNK):
        qkv = dot(left_qkv, features_of(normed_refs, first, side)).astype(BF16)
        out = dot(left_out, features_of([cot_ref], first, side)).astype(BF16)
        groups = [qkv[:HD], qkv[HD : 2 * HD], qkv[2 * HD :], out]
        for block in range(CHUNK):
            columns = slice(block * HD, (block + 1) * HD)
            values = [value[:, columns] for value in groups]
            first_ref[first + block] = pick(values, x)
            for step in range(1, GROUPS):
                rest_ref[step - 1, first + block] = pick(values[step:] + values[:step], x)


def attention_kernel(place_ref, band_ref, normed_ref, low_ref, high_ref, cot_ref, *refs):
    own, other = refs[:GROUPS], refs[GROUPS : 2 * GROUPS]
    (
        away_first_ref,
        away_rest_ref,
        left_qkv_ref,
        left_out_ref,
        own_grads_ref,
        low_back_ref,
        high_back_ref,
        proj,
        datt,
    ) = refs[2 * GROUPS :]
    x = place_ref[0]
    core = place_ref[1]
    normed_refs = [normed_ref, low_ref, high_ref]

    for position in range(GROUPS):
        steps = [(position - group) % GROUPS for group in range(GROUPS)]

        @pl.when(x == position)
        def _():
            proj[...] = project(
                normed_refs,
                (
                    columns_of([own[step] for step in steps[:3]]),
                    columns_of([other[step] for step in steps[:3]]),
                ),
                core,
            )
            datt[...] = project_back([cot_ref], (own[steps[3]], other[steps[3]]), core)

    queries = proj[:ROWS, :HD]
    keys = proj[:, HD : 2 * HD]
    values = proj[:, 2 * HD :]
    d_att = datt[...]
    place = lax.broadcasted_iota(jnp.int32, (1, EXT), 1)
    column = (place - ROWS) % HALO
    low = (place >= ROWS) & (place < ROWS + EDGE)
    high = (place >= ROWS + PAD) & (place < ROWS + PAD + EDGE)
    usable = (
        (place < ROWS)
        | (low & (HALO - column <= band_ref[0, 0]))
        | (high & (column + 1 <= band_ref[0, 1]))
    )
    scale = HD ** (-0.5)
    scores = jnp.where(usable, dot(queries, keys, OVER_COLS) * scale, -jnp.inf)
    exp_scores = jnp.exp(scores - jnp.max(scores, axis=-1, keepdims=True))
    probs = exp_scores / jnp.sum(exp_scores, axis=-1, keepdims=True)
    probs_low = probs.astype(BF16)
    attended = dot(probs_low, values).astype(BF16)
    d_probs = dot(d_att, values, OVER_COLS)
    inner = jnp.sum(probs * d_probs, axis=-1, keepdims=True)
    d_scores = (probs * (d_probs - inner) * scale).astype(BF16)
    d_query = dot(d_scores, keys)
    d_keys = dot(d_scores, queries, OVER_ROWS)
    d_values = dot(probs_low, d_att, OVER_ROWS)
    own_grads_ref[:, :HD] = d_query
    own_grads_ref[:, HD : 2 * HD] = d_keys[:ROWS]
    own_grads_ref[:, 2 * HD :] = d_values[:ROWS]
    for ref, start in ((low_back_ref, ROWS), (high_back_ref, ROWS + PAD)):
        ref[:, :HD] = d_keys[start : start + PAD].astype(BF16)
        ref[:, HD:] = d_values[start : start + PAD].astype(BF16)
    d_query_ext = jnp.concatenate([d_query, jnp.zeros((2 * PAD, HD), F32)], axis=0)
    left_qkv = jnp.concatenate([d_query_ext.T, d_keys.T, d_values.T], axis=0).astype(BF16)
    left_out = attended.astype(F32).T.astype(BF16)
    left_qkv_ref[...] = left_qkv
    left_out_ref[...] = left_out
    store_grads(
        away_first_ref, away_rest_ref, left_qkv, left_out, normed_refs, cot_ref, x, 1 - core
    )


def own_half_kernel(place_ref, left_qkv_ref, left_out_ref, *refs):
    normed_refs, cot_ref, first_ref, rest_ref = refs[:3], refs[3], refs[4], refs[5]
    store_grads(
        first_ref,
        rest_ref,
        left_qkv_ref[...],
        left_out_ref[...],
        normed_refs,
        cot_ref,
        place_ref[0],
        place_ref[1],
    )


def spread_kernel(place_ref, w_qkv_ref, w_out_ref, out_ref, qkv_block, out_block, sems):
    copies = [
        pltpu.make_async_copy(w_qkv_ref, qkv_block, sems.at[0]),
        pltpu.make_async_copy(w_out_ref, out_block, sems.at[1]),
    ]
    for copy in copies:
        copy.start()
    for copy in copies:
        copy.wait()
    columns = [qkv_block[:, group * HD : (group + 1) * HD] for group in range(3)]
    mine = pick(columns + [out_block[...]], place_ref[0])
    for block in range(BLOCKS):
        out_ref[block] = mine


def piece_kernel(pieces_ref, out_ref):
    total = pieces_ref[0].astype(F32)
    for source in range(1, pieces_ref.shape[0]):
        total = total + pieces_ref[source].astype(F32)
    total = total.astype(BF16)
    for target in range(out_ref.shape[0]):
        out_ref[target] = total


def final_kernel(full_ref, qkv_ref, out_ref):
    for group in range(GROUPS):
        value = jnp.concatenate(
            [full_ref[4 * quarter + group].astype(F32) for quarter in range(4)], axis=0
        )
        if group < 3:
            qkv_ref[:, group * HD : (group + 1) * HD] = value.T
        else:
            out_ref[...] = value


def line_kernel(*refs):
    for block in range(BLOCKS):
        total = refs[0][block].astype(F32)
        for ref in refs[1:-1]:
            total = total + ref[block].astype(F32)
        total = total.astype(BF16)
        for quarter in range(4):
            refs[-1][quarter, block] = total[quarter * 32 : (quarter + 1) * 32]


def tokens_kernel(
    place_ref, grads_ref, from_left_ref, from_right_ref, tokens_ref, inverse_ref, *refs
):
    own, other = refs[:GROUPS], refs[GROUPS : 2 * GROUPS]
    out_ref, d_normed, d_qkv = refs[2 * GROUPS :]
    x = place_ref[0]
    core = place_ref[1]
    first, last = edge_chooser((ROWS, PAD), 0)
    d_kv = (
        grads_ref[:, HD:]
        + dot(as_weights(first), from_left_ref[...])
        + dot(as_weights(last), from_right_ref[...])
    )
    d_qkv[0] = grads_ref[:, :HD].astype(BF16)
    d_qkv[1] = d_kv[:, :HD].astype(BF16)
    d_qkv[2] = d_kv[:, HD:].astype(BF16)
    d_qkv[3] = jnp.zeros((ROWS, HD), BF16)
    left = jnp.concatenate(
        [d_qkv[(x - step + GROUPS) % GROUPS] for step in range(GROUPS)], axis=1
    )
    total = jnp.zeros((ROWS, HD), F32)
    for parts, side in ((own, core), (other, 1 - core)):
        for block in range(BLOCKS):
            weights = jnp.concatenate([part[block] for part in parts], axis=1)
            piece = dot(left, weights, OVER_COLS)
            columns = feature_block(block, side)
            d_normed[:, columns] = piece
            total = total + piece * tokens_ref[:, columns].astype(F32)
    inverse = inverse_ref[...]
    mean = jnp.sum(total, axis=-1, keepdims=True) * (1.0 / (2 * BLOCKS * HD))
    factor = inverse * inverse * inverse * mean
    for block in range(2 * BLOCKS):
        columns = slice(block * HD, (block + 1) * HD)
        out_ref[:, columns] = (
            inverse * d_normed[:, columns] - tokens_ref[:, columns].astype(F32) * factor
        ).astype(BF16)


def call(body, operands, outs, scratch, flops, in_bytes, smem):
    whole = pl.BlockSpec(memory_space=pltpu.VMEM)
    scalars = pl.BlockSpec(memory_space=pltpu.SMEM)
    return pl.pallas_call(
        body,
        in_specs=[scalars] * smem + [whole] * (len(operands) - smem),
        out_specs=[whole] * len(outs),
        out_shape=[jax.ShapeDtypeStruct(shape, dtype) for shape, dtype in outs],
        scratch_shapes=[pltpu.VMEM(shape, dtype) for shape, dtype in scratch],
        compiler_params=pltpu.CompilerParams(vmem_limit_bytes=VMEM_BYTES),
        cost_estimate=pl.CostEstimate(
            flops=flops, bytes_accessed=in_bytes, transcendentals=0
        ),
    )(*operands)


def mirrored_groups():
    return [
        [y * 8 + (3 - zlo if zhi else zlo) * 2 + zhi for zhi in range(2) for y in range(8)]
        for zlo in range(4)
    ]


def local(tokens, w_qkv, w_out, band, cotangent):
    samples, lat_rows, lon_cols, features = tokens.shape
    place = jnp.stack([lax.axis_index("x"), lax.axis_index("core")]).astype(jnp.int32)
    forward = shift_pairs(16, 1)
    backward = shift_pairs(16, -1)
    swap = shift_pairs(2, 1)
    tok_rows = tokens.reshape(ROWS, features)
    cot_rows = cotangent.reshape(ROWS, features)
    spread = pl.pallas_call(
        spread_kernel,
        in_specs=[
            pl.BlockSpec(memory_space=pltpu.SMEM),
            pl.BlockSpec(memory_space=pl.ANY),
            pl.BlockSpec(memory_space=pl.ANY),
        ],
        out_specs=pl.BlockSpec(memory_space=pltpu.VMEM),
        out_shape=jax.ShapeDtypeStruct((BLOCKS, HD, HD), BF16),
        scratch_shapes=[
            pltpu.VMEM((HD, 3 * HD), BF16),
            pltpu.VMEM((HD, HD), BF16),
            pltpu.SemaphoreType.DMA((2,)),
        ],
        compiler_params=pltpu.CompilerParams(vmem_limit_bytes=VMEM_BYTES),
        cost_estimate=pl.CostEstimate(flops=0, bytes_accessed=700_000, transcendentals=0),
    )(place, w_qkv, w_out)
    spread = lax.all_to_all(
        spread, ("y", "zlo", "zhi"), 0, 0, axis_index_groups=mirrored_groups()
    )
    steps = {step: lax.ppermute(spread, "x", shift_pairs(GROUPS, step)) for step in STEPS}
    own = [spread, steps[1], steps[2], steps[3]]
    late_rows, unused = lax.optimization_barrier((tok_rows, spread))
    normed_own, inverse, first, last = call(
        normalise_kernel,
        [late_rows],
        [
            ((ROWS, features), BF16),
            ((ROWS, 1), F32),
            ((PAD, features), BF16),
            ((PAD, features), BF16),
        ],
        [],
        200_000_000,
        3_000_000,
        0,
    )
    low = lax.ppermute(last, TILE, forward)
    high = lax.ppermute(first, TILE, backward)
    own[2], low, high = lax.optimization_barrier((own[2], low, high))
    normed = [normed_own, low, high]
    other = [lax.ppermute(part, "core", swap) for part in own]

    first_shape = ((BLOCKS, HD, HD), BF16)
    rest_shape = ((GROUPS - 1, BLOCKS, HD, HD), BF16)
    away_first, away_rest, left_qkv, left_out, own_grads, low_back, high_back = call(
        attention_kernel,
        [place, band, *normed, cot_rows, *own, *other],
        [
            first_shape,
            rest_shape,
            ((3 * HD, EXT), BF16),
            ((HD, ROWS), BF16),
            ((ROWS, 3 * HD), F32),
            ((PAD, 2 * HD), BF16),
            ((PAD, 2 * HD), BF16),
        ],
        [((EXT, 3 * HD), BF16), ((ROWS, HD), BF16)],
        3_000_000_000,
        12_000_000,
        2,
    )
    got_rest = lax.ppermute(away_rest, "core", swap)
    got_first = lax.ppermute(away_first, "core", swap)
    kept_first, kept_rest = call(
        own_half_kernel,
        [place, left_qkv, left_out, *normed, cot_rows],
        [first_shape, rest_shape],
        [],
        500_000_000,
        6_000_000,
        1,
    )
    sent = [
        (kept_rest[step].astype(F32) + got_rest[step].astype(F32)).astype(BF16)
        for step in range(GROUPS - 1)
    ]
    sent, low_back, high_back = lax.optimization_barrier((sent, low_back, high_back))
    arrived = [
        lax.ppermute(sent[step - 1], "x", shift_pairs(GROUPS, step)) for step in STEPS
    ]
    from_right = lax.ppermute(low_back, TILE, backward)
    from_left = lax.ppermute(high_back, TILE, forward)
    from_left, from_right = lax.optimization_barrier((from_left, from_right))
    (d_tokens,) = call(
        tokens_kernel,
        [place, own_grads, from_left, from_right, tok_rows, inverse, *own, *other],
        [((ROWS, features), BF16)],
        [((ROWS, features), F32), ((GROUPS, ROWS, HD), BF16)],
        800_000_000,
        8_000_000,
        1,
    )
    (line,) = call(
        line_kernel,
        [kept_first, got_first, *arrived],
        [((4, BLOCKS, 32, HD), BF16)],
        [],
        2_000_000,
        3_000_000,
        0,
    )
    line, d_tokens = lax.optimization_barrier((line, d_tokens))
    pieces = lax.all_to_all(line.reshape(64, 32, HD), ("zlo", "zhi", "y"), 0, 0)
    (piece,) = call(
        piece_kernel, [pieces], [((16, 32, HD), BF16)], [], 1_000_000, 1_000_000, 0
    )
    full = lax.all_to_all(piece, ("zlo", "x"), 0, 0)
    grad_qkv, grad_out = call(
        final_kernel, [full], [((HD, 3 * HD), F32), ((HD, HD), F32)], [], 1_000_000, 500_000, 0
    )
    return (d_tokens.reshape(tokens.shape), grad_qkv, grad_out)


def solution(mesh):
    inner = jax.sharding.Mesh(
        mesh.devices.reshape(4, 4, 8, 2, 2), ("x", "zlo", "y", "zhi", "core")
    )
    placed = (
        P(FSDP, None, TILE, None),
        P(FSDP, None),
        P(None, FSDP),
        P(TILE, None),
        P(FSDP, None, TILE, None),
    )
    return jax.shard_map(
        local,
        mesh=inner,
        in_specs=placed,
        out_specs=(P(FSDP, None, TILE, None), P(FSDP, None), P(None, FSDP)),
        check_vma=False,
    )
```

```python
import functools

import jax
import jax.numpy as jnp
from jax import lax
from jax.experimental import pallas as pl
from jax.experimental.pallas import tpu as pltpu
from jax.sharding import PartitionSpec as P

HALO = 2
EPS = 1e-05
TILE = ("x", "zlo")
FSDP = ("y", "zhi", "core")
GROUPS = 4
HD = 128
ROWS = 192
EDGE = 24
PAD = 32
EXT = ROWS + 2 * PAD
STEPS = (2, 1, 3)
BLOCKS = 16
CHUNK = 4
VMEM_BYTES = 40 * 1024 * 1024
OVER_ROWS = (((0,), (0,)), ((), ()))
OVER_COLS = (((1,), (1,)), ((), ()))
F32 = jnp.float32
BF16 = jnp.bfloat16


def shift_pairs(count, step):
    return [(i, (i + step) % count) for i in range(count)]


def dot(a, b, dims=(((1,), (0,)), ((), ()))):
    return lax.dot_general(a, b, dims, preferred_element_type=F32)


def feature_block(block, core):
    zhi, y = divmod(block, 8)
    return pl.ds(pl.multiple_of((2 * (2 * y + zhi) + core) * HD, HD), HD)


def features_of(refs, first, core):
    columns = [
        jnp.concatenate([ref[:, feature_block(block, core)] for ref in refs], axis=0)
        for block in range(first, first + CHUNK)
    ]
    return jnp.concatenate(columns, axis=1)


def edge_chooser(shape, row_axis):
    row = lax.broadcasted_iota(jnp.int32, shape, row_axis)
    edge = lax.broadcasted_iota(jnp.int32, shape, 1 - row_axis)
    column = row % 16
    base = (row // 16) * HALO
    last = (column >= 16 - HALO) & (edge == base + column - (16 - HALO))
    first = (column < HALO) & (edge == base + column)
    return first, last


def as_weights(mask):
    return jnp.where(mask, 1.0, 0.0).astype(BF16)


def normalise_kernel(tokens_ref, normed_ref, inverse_ref, first_ref, last_ref):
    total = jnp.zeros((ROWS, HD), F32)
    for block in range(2 * BLOCKS):
        piece = tokens_ref[:, block * HD : (block + 1) * HD].astype(F32)
        total = total + piece * piece
    mean = jnp.sum(total, axis=-1, keepdims=True) * (1.0 / (2 * BLOCKS * HD))
    inverse = lax.rsqrt(mean + EPS)
    inverse_ref[...] = inverse
    first, last = edge_chooser((PAD, ROWS), 1)
    first, last = as_weights(first), as_weights(last)
    for block in range(0, 2 * BLOCKS, CHUNK):
        columns = slice(block * HD, (block + CHUNK) * HD)
        piece = (tokens_ref[:, columns].astype(F32) * inverse).astype(BF16)
        normed_ref[:, columns] = piece
        first_ref[:, columns] = dot(first, piece).astype(BF16)
        last_ref[:, columns] = dot(last, piece).astype(BF16)


def project(rows_refs, parts, core):
    total = None
    for part, side in zip(parts, (core, 1 - core)):
        for first in range(0, BLOCKS, CHUNK):
            term = dot(features_of(rows_refs, first, side), part(first))
            total = term if total is None else total + term
    return total.astype(BF16)


def columns_of(refs):
    def weights(first):
        return jnp.concatenate(
            [ref[first : first + CHUNK].reshape(CHUNK * HD, HD) for ref in refs], axis=1
        )

    return weights


def pick(values, index):
    chosen = values[0]
    for place in range(1, len(values)):
        chosen = jnp.where(index == place, values[place], chosen)
    return chosen


def project_back(rows_refs, parts, core):
    total = None
    for ref, side in zip(parts, (core, 1 - core)):
        for first in range(0, BLOCKS, CHUNK):
            blocks = [ref[block] for block in range(first, first + CHUNK)]
            term = dot(
                features_of(rows_refs, first, side), jnp.concatenate(blocks, axis=1), OVER_COLS
            )
            total = term if total is None else total + term
    return total.astype(BF16)


def store_grads(first_ref, rest_ref, left_qkv, left_out, normed_refs, cot_ref, x, side):
    for first in range(0, BLOCKS, CHUNK):
        qkv = dot(left_qkv, features_of(normed_refs, first, side)).astype(BF16)
        out = dot(left_out, features_of([cot_ref], first, side)).astype(BF16)
        groups = [qkv[:HD], qkv[HD : 2 * HD], qkv[2 * HD :], out]
        for block in range(CHUNK):
            columns = slice(block * HD, (block + 1) * HD)
            values = [value[:, columns] for value in groups]
            first_ref[first + block] = pick(values, x)
            for step in range(1, GROUPS):
                rest_ref[step - 1, first + block] = pick(values[step:] + values[:step], x)


def attention_kernel(place_ref, band_ref, normed_ref, low_ref, high_ref, cot_ref, *refs):
    own, other = refs[:GROUPS], refs[GROUPS : 2 * GROUPS]
    (
        away_first_ref,
        away_rest_ref,
        left_qkv_ref,
        left_out_ref,
        own_grads_ref,
        low_back_ref,
        high_back_ref,
        proj,
        datt,
    ) = refs[2 * GROUPS :]
    x = place_ref[0]
    core = place_ref[1]
    normed_refs = [normed_ref, low_ref, high_ref]

    for position in range(GROUPS):
        steps = [(position - group) % GROUPS for group in range(GROUPS)]

        @pl.when(x == position)
        def _():
            proj[...] = project(
                normed_refs,
                (
                    columns_of([own[step] for step in steps[:3]]),
                    columns_of([other[step] for step in steps[:3]]),
                ),
                core,
            )
            datt[...] = project_back([cot_ref], (own[steps[3]], other[steps[3]]), core)

    queries = proj[:ROWS, :HD]
    keys = proj[:, HD : 2 * HD]
    values = proj[:, 2 * HD :]
    d_att = datt[...]
    place = lax.broadcasted_iota(jnp.int32, (1, EXT), 1)
    column = (place - ROWS) % HALO
    low = (place >= ROWS) & (place < ROWS + EDGE)
    high = (place >= ROWS + PAD) & (place < ROWS + PAD + EDGE)
    usable = (
        (place < ROWS)
        | (low & (HALO - column <= band_ref[0, 0]))
        | (high & (column + 1 <= band_ref[0, 1]))
    )
    scale = HD ** (-0.5)
    scores = jnp.where(usable, dot(queries, keys, OVER_COLS) * scale, -jnp.inf)
    exp_scores = jnp.exp(scores - jnp.max(scores, axis=-1, keepdims=True))
    probs = exp_scores / jnp.sum(exp_scores, axis=-1, keepdims=True)
    probs_low = probs.astype(BF16)
    attended = dot(probs_low, values).astype(BF16)
    d_probs = dot(d_att, values, OVER_COLS)
    inner = jnp.sum(probs * d_probs, axis=-1, keepdims=True)
    d_scores = (probs * (d_probs - inner) * scale).astype(BF16)
    d_query = dot(d_scores, keys)
    d_keys = dot(d_scores, queries, OVER_ROWS)
    d_values = dot(probs_low, d_att, OVER_ROWS)
    own_grads_ref[:, :HD] = d_query
    own_grads_ref[:, HD : 2 * HD] = d_keys[:ROWS]
    own_grads_ref[:, 2 * HD :] = d_values[:ROWS]
    for ref, start in ((low_back_ref, ROWS), (high_back_ref, ROWS + PAD)):
        ref[:, :HD] = d_keys[start : start + PAD].astype(BF16)
        ref[:, HD:] = d_values[start : start + PAD].astype(BF16)
    d_query_ext = jnp.concatenate([d_query, jnp.zeros((2 * PAD, HD), F32)], axis=0)
    left_qkv = jnp.concatenate([d_query_ext.T, d_keys.T, d_values.T], axis=0).astype(BF16)
    left_out = attended.astype(F32).T.astype(BF16)
    left_qkv_ref[...] = left_qkv
    left_out_ref[...] = left_out
    store_grads(
        away_first_ref, away_rest_ref, left_qkv, left_out, normed_refs, cot_ref, x, 1 - core
    )


def own_half_kernel(place_ref, left_qkv_ref, left_out_ref, *refs):
    normed_refs, cot_ref, first_ref, rest_ref = refs[:3], refs[3], refs[4], refs[5]
    store_grads(
        first_ref,
        rest_ref,
        left_qkv_ref[...],
        left_out_ref[...],
        normed_refs,
        cot_ref,
        place_ref[0],
        place_ref[1],
    )


def spread_kernel(place_ref, w_qkv_ref, w_out_ref, out_ref, qkv_block, out_block, sems):
    copies = [
        pltpu.make_async_copy(w_qkv_ref, qkv_block, sems.at[0]),
        pltpu.make_async_copy(w_out_ref, out_block, sems.at[1]),
    ]
    for copy in copies:
        copy.start()
    for copy in copies:
        copy.wait()
    columns = [qkv_block[:, group * HD : (group + 1) * HD] for group in range(3)]
    mine = pick(columns + [out_block[...]], place_ref[0])
    for block in range(BLOCKS):
        out_ref[block] = mine


def piece_kernel(pieces_ref, out_ref):
    total = pieces_ref[0].astype(F32)
    for source in range(1, pieces_ref.shape[0]):
        total = total + pieces_ref[source].astype(F32)
    total = total.astype(BF16)
    for target in range(out_ref.shape[0]):
        out_ref[target] = total


def final_kernel(full_ref, qkv_ref, out_ref):
    for group in range(GROUPS):
        value = jnp.concatenate(
            [
                full_ref[4 * quarter + (group - 2 * inner_line(quarter)) % GROUPS].astype(F32)
                for quarter in range(4)
            ],
            axis=0,
        )
        if group < 3:
            qkv_ref[:, group * HD : (group + 1) * HD] = value.T
        else:
            out_ref[...] = value


def line_kernel(*refs):
    for block in range(BLOCKS):
        total = refs[0][block].astype(F32)
        for ref in refs[1:-1]:
            total = total + ref[block].astype(F32)
        total = total.astype(BF16)
        for quarter in range(4):
            refs[-1][quarter, block] = total[quarter * 32 : (quarter + 1) * 32]


def tokens_kernel(
    place_ref, grads_ref, from_left_ref, from_right_ref, tokens_ref, inverse_ref, *refs
):
    own, other = refs[:GROUPS], refs[GROUPS : 2 * GROUPS]
    out_ref, d_normed, d_qkv = refs[2 * GROUPS :]
    x = place_ref[0]
    core = place_ref[1]
    first, last = edge_chooser((ROWS, PAD), 0)
    d_kv = (
        grads_ref[:, HD:]
        + dot(as_weights(first), from_left_ref[...])
        + dot(as_weights(last), from_right_ref[...])
    )
    d_qkv[0] = grads_ref[:, :HD].astype(BF16)
    d_qkv[1] = d_kv[:, :HD].astype(BF16)
    d_qkv[2] = d_kv[:, HD:].astype(BF16)
    d_qkv[3] = jnp.zeros((ROWS, HD), BF16)
    left = jnp.concatenate(
        [d_qkv[(x - step + GROUPS) % GROUPS] for step in range(GROUPS)], axis=1
    )
    total = jnp.zeros((ROWS, HD), F32)
    for parts, side in ((own, core), (other, 1 - core)):
        for block in range(BLOCKS):
            weights = jnp.concatenate([part[block] for part in parts], axis=1)
            piece = dot(left, weights, OVER_COLS)
            columns = feature_block(block, side)
            d_normed[:, columns] = piece
            total = total + piece * tokens_ref[:, columns].astype(F32)
    inverse = inverse_ref[...]
    mean = jnp.sum(total, axis=-1, keepdims=True) * (1.0 / (2 * BLOCKS * HD))
    factor = inverse * inverse * inverse * mean
    for block in range(2 * BLOCKS):
        columns = slice(block * HD, (block + 1) * HD)
        out_ref[:, columns] = (
            inverse * d_normed[:, columns] - tokens_ref[:, columns].astype(F32) * factor
        ).astype(BF16)


def call(body, operands, outs, scratch, flops, in_bytes, smem):
    whole = pl.BlockSpec(memory_space=pltpu.VMEM)
    scalars = pl.BlockSpec(memory_space=pltpu.SMEM)
    return pl.pallas_call(
        body,
        in_specs=[scalars] * smem + [whole] * (len(operands) - smem),
        out_specs=[whole] * len(outs),
        out_shape=[jax.ShapeDtypeStruct(shape, dtype) for shape, dtype in outs],
        scratch_shapes=[pltpu.VMEM(shape, dtype) for shape, dtype in scratch],
        compiler_params=pltpu.CompilerParams(vmem_limit_bytes=VMEM_BYTES),
        cost_estimate=pl.CostEstimate(
            flops=flops, bytes_accessed=in_bytes, transcendentals=0
        ),
    )(*operands)


def inner_line(zlo):
    return (zlo + 1) // 2 % 2


def send(value, step):
    if step == 2:
        return lax.ppermute(value, "zlo", [(0, 1), (1, 0), (2, 3), (3, 2)])
    return lax.ppermute(value, "x", shift_pairs(GROUPS, step))


def line_groups():
    return [
        [
            (((held - 2 * inner_line(zlo)) % GROUPS * 8 + y) * 4 + zlo) * 2 + zhi
            for zlo in range(4)
            for zhi in range(2)
            for y in range(8)
        ]
        for held in range(GROUPS)
    ]


def mirrored_groups():
    return [
        [y * 8 + (3 - zlo if zhi else zlo) * 2 + zhi for zhi in range(2) for y in range(8)]
        for zlo in range(4)
    ]


def local(tokens, w_qkv, w_out, band, cotangent):
    samples, lat_rows, lon_cols, features = tokens.shape
    held = (lax.axis_index("x") + 2 * inner_line(lax.axis_index("zlo"))) % GROUPS
    place = jnp.stack([held, lax.axis_index("core")]).astype(jnp.int32)
    forward = shift_pairs(16, 1)
    backward = shift_pairs(16, -1)
    swap = shift_pairs(2, 1)
    tok_rows = tokens.reshape(ROWS, features)
    cot_rows = cotangent.reshape(ROWS, features)
    spread = pl.pallas_call(
        spread_kernel,
        in_specs=[
            pl.BlockSpec(memory_space=pltpu.SMEM),
            pl.BlockSpec(memory_space=pl.ANY),
            pl.BlockSpec(memory_space=pl.ANY),
        ],
        out_specs=pl.BlockSpec(memory_space=pltpu.VMEM),
        out_shape=jax.ShapeDtypeStruct((BLOCKS, HD, HD), BF16),
        scratch_shapes=[
            pltpu.VMEM((HD, 3 * HD), BF16),
            pltpu.VMEM((HD, HD), BF16),
            pltpu.SemaphoreType.DMA((2,)),
        ],
        compiler_params=pltpu.CompilerParams(vmem_limit_bytes=VMEM_BYTES),
        cost_estimate=pl.CostEstimate(flops=0, bytes_accessed=700_000, transcendentals=0),
    )(place, w_qkv, w_out)
    spread = lax.all_to_all(
        spread, ("y", "zlo", "zhi"), 0, 0, axis_index_groups=mirrored_groups()
    )
    steps = {step: send(spread, step) for step in STEPS}
    own = [spread, steps[1], steps[2], steps[3]]
    passed = lax.ppermute(spread, "core", swap)
    late_rows, passed = lax.optimization_barrier((tok_rows, passed))
    normed_own, inverse, first, last = call(
        normalise_kernel,
        [late_rows],
        [
            ((ROWS, features), BF16),
            ((ROWS, 1), F32),
            ((PAD, features), BF16),
            ((PAD, features), BF16),
        ],
        [],
        200_000_000,
        3_000_000,
        0,
    )
    low = lax.ppermute(last, TILE, forward)
    high = lax.ppermute(first, TILE, backward)
    own[3], low, high = lax.optimization_barrier((own[3], low, high))
    normed = [normed_own, low, high]
    other = [passed] + [lax.ppermute(part, "core", swap) for part in own[1:]]

    first_shape = ((BLOCKS, HD, HD), BF16)
    rest_shape = ((GROUPS - 1, BLOCKS, HD, HD), BF16)
    away_first, away_rest, left_qkv, left_out, own_grads, low_back, high_back = call(
        attention_kernel,
        [place, band, *normed, cot_rows, *own, *other],
        [
            first_shape,
            rest_shape,
            ((3 * HD, EXT), BF16),
            ((HD, ROWS), BF16),
            ((ROWS, 3 * HD), F32),
            ((PAD, 2 * HD), BF16),
            ((PAD, 2 * HD), BF16),
        ],
        [((EXT, 3 * HD), BF16), ((ROWS, HD), BF16)],
        3_000_000_000,
        12_000_000,
        2,
    )
    got_rest = lax.ppermute(away_rest, "core", swap)
    got_first = lax.ppermute(away_first, "core", swap)
    kept_first, kept_rest = call(
        own_half_kernel,
        [place, left_qkv, left_out, *normed, cot_rows],
        [first_shape, rest_shape],
        [],
        500_000_000,
        6_000_000,
        1,
    )
    sent = [
        (kept_rest[step].astype(F32) + got_rest[step].astype(F32)).astype(BF16)
        for step in range(GROUPS - 1)
    ]
    arrived = [
        send(sent[step - 1], step) for step in STEPS
    ]
    from_right = lax.ppermute(low_back, TILE, backward)
    from_left = lax.ppermute(high_back, TILE, forward)
    (line,) = call(
        line_kernel,
        [kept_first, got_first, *arrived],
        [((4, BLOCKS, 32, HD), BF16)],
        [],
        2_000_000,
        3_000_000,
        0,
    )
    line, from_left, from_right = lax.optimization_barrier((line, from_left, from_right))
    pieces = lax.all_to_all(
        line.reshape(64, 32, HD),
        ("x", "y", "zlo", "zhi"),
        0,
        0,
        axis_index_groups=line_groups(),
    )
    (d_tokens,) = call(
        tokens_kernel,
        [place, own_grads, from_left, from_right, tok_rows, inverse, *own, *other],
        [((ROWS, features), BF16)],
        [((ROWS, features), F32), ((GROUPS, ROWS, HD), BF16)],
        800_000_000,
        8_000_000,
        1,
    )
    pieces, d_tokens = lax.optimization_barrier((pieces, d_tokens))
    (piece,) = call(
        piece_kernel, [pieces], [((16, 32, HD), BF16)], [], 1_000_000, 1_000_000, 0
    )
    full = lax.all_to_all(piece, ("zlo", "x"), 0, 0)
    grad_qkv, grad_out = call(
        final_kernel, [full], [((HD, 3 * HD), F32), ((HD, HD), F32)], [], 1_000_000, 500_000, 0
    )
    return (d_tokens.reshape(tokens.shape), grad_qkv, grad_out)


def solution(mesh):
    inner = jax.sharding.Mesh(
        mesh.devices.reshape(4, 4, 8, 2, 2), ("x", "zlo", "y", "zhi", "core")
    )
    placed = (
        P(FSDP, None, TILE, None),
        P(FSDP, None),
        P(None, FSDP),
        P(TILE, None),
        P(FSDP, None, TILE, None),
    )
    return jax.shard_map(
        local,
        mesh=inner,
        in_specs=placed,
        out_specs=(P(FSDP, None, TILE, None), P(FSDP, None), P(None, FSDP)),
        check_vma=False,
    )
```

```python
import functools

import jax
import jax.numpy as jnp
from jax import lax
from jax.experimental import pallas as pl
from jax.experimental.pallas import tpu as pltpu
from jax.sharding import PartitionSpec as P

HALO = 2
EPS = 1e-05
TILE = ("x", "zlo")
FSDP = ("y", "zhi", "core")
GROUPS = 4
HD = 128
ROWS = 192
EDGE = 24
PAD = 32
SENT = 24
EXT = ROWS + 2 * SENT
STEPS = (2, 1, 3)
BLOCKS = 16
CHUNK = 4
VMEM_BYTES = 40 * 1024 * 1024
OVER_ROWS = (((0,), (0,)), ((), ()))
OVER_COLS = (((1,), (1,)), ((), ()))
F32 = jnp.float32
BF16 = jnp.bfloat16


def shift_pairs(count, step):
    return [(i, (i + step) % count) for i in range(count)]


def dot(a, b, dims=(((1,), (0,)), ((), ()))):
    return lax.dot_general(a, b, dims, preferred_element_type=F32)


def feature_block(block, core):
    zhi, y = divmod(block, 8)
    return pl.ds(pl.multiple_of((2 * (2 * y + zhi) + core) * HD, HD), HD)


def features_of(refs, first, core):
    columns = [
        jnp.concatenate([ref[:, feature_block(block, core)] for ref in refs], axis=0)
        for block in range(first, first + CHUNK)
    ]
    return jnp.concatenate(columns, axis=1)


def edge_chooser(shape, row_axis):
    row = lax.broadcasted_iota(jnp.int32, shape, row_axis)
    edge = lax.broadcasted_iota(jnp.int32, shape, 1 - row_axis)
    column = row % 16
    base = (row // 16) * HALO
    last = (column >= 16 - HALO) & (edge == base + column - (16 - HALO))
    first = (column < HALO) & (edge == base + column)
    return first, last


def as_weights(mask):
    return jnp.where(mask, 1.0, 0.0).astype(BF16)


def normalise_kernel(tokens_ref, normed_ref, inverse_ref, first_ref, last_ref):
    total = jnp.zeros((ROWS, HD), F32)
    for block in range(2 * BLOCKS):
        piece = tokens_ref[:, block * HD : (block + 1) * HD].astype(F32)
        total = total + piece * piece
    mean = jnp.sum(total, axis=-1, keepdims=True) * (1.0 / (2 * BLOCKS * HD))
    inverse = lax.rsqrt(mean + EPS)
    inverse_ref[...] = inverse
    first, last = edge_chooser((SENT, ROWS), 1)
    first, last = as_weights(first), as_weights(last)
    for block in range(0, 2 * BLOCKS, CHUNK):
        columns = slice(block * HD, (block + CHUNK) * HD)
        piece = (tokens_ref[:, columns].astype(F32) * inverse).astype(BF16)
        normed_ref[:, columns] = piece
        first_ref[:, columns] = dot(first, piece).astype(BF16)
        last_ref[:, columns] = dot(last, piece).astype(BF16)


def project(rows_refs, parts, core):
    total = None
    for part, side in zip(parts, (core, 1 - core)):
        for first in range(0, BLOCKS, CHUNK):
            term = dot(features_of(rows_refs, first, side), part(first))
            total = term if total is None else total + term
    return total.astype(BF16)


def columns_of(refs):
    def weights(first):
        return jnp.concatenate(
            [ref[first : first + CHUNK].reshape(CHUNK * HD, HD) for ref in refs], axis=1
        )

    return weights


def pick(values, index):
    chosen = values[0]
    for place in range(1, len(values)):
        chosen = jnp.where(index == place, values[place], chosen)
    return chosen


def project_back(rows_refs, parts, core):
    total = None
    for ref, side in zip(parts, (core, 1 - core)):
        for first in range(0, BLOCKS, CHUNK):
            blocks = [ref[block] for block in range(first, first + CHUNK)]
            term = dot(
                features_of(rows_refs, first, side), jnp.concatenate(blocks, axis=1), OVER_COLS
            )
            total = term if total is None else total + term
    return total.astype(BF16)


def store_grads(first_ref, rest_ref, left_qkv, left_out, normed_refs, cot_ref, x, side):
    for first in range(0, BLOCKS, CHUNK):
        qkv = dot(left_qkv, features_of(normed_refs, first, side)).astype(BF16)
        out = dot(left_out, features_of([cot_ref], first, side)).astype(BF16)
        groups = [qkv[:HD], qkv[HD : 2 * HD], qkv[2 * HD :], out]
        for block in range(CHUNK):
            columns = slice(block * HD, (block + 1) * HD)
            values = [value[:, columns] for value in groups]
            first_ref[first + block] = pick(values, x)
            for step in range(1, GROUPS):
                rest_ref[step - 1, first + block] = pick(values[step:] + values[:step], x)


def attention_kernel(place_ref, band_ref, normed_ref, low_ref, high_ref, cot_ref, *refs):
    own, other = refs[:GROUPS], refs[GROUPS : 2 * GROUPS]
    (
        away_first_ref,
        away_rest_ref,
        left_qkv_ref,
        left_out_ref,
        own_grads_ref,
        low_back_ref,
        high_back_ref,
        proj,
        datt,
    ) = refs[2 * GROUPS :]
    x = place_ref[0]
    core = place_ref[1]
    normed_refs = [normed_ref, low_ref, high_ref]

    for position in range(GROUPS):
        steps = [(position - group) % GROUPS for group in range(GROUPS)]

        @pl.when(x == position)
        def _():
            proj[...] = project(
                normed_refs,
                (
                    columns_of([own[step] for step in steps[:3]]),
                    columns_of([other[step] for step in steps[:3]]),
                ),
                core,
            )
            datt[...] = project_back([cot_ref], (own[steps[3]], other[steps[3]]), core)

    queries = proj[:ROWS, :HD]
    keys = proj[:, HD : 2 * HD]
    values = proj[:, 2 * HD :]
    d_att = datt[...]
    place = lax.broadcasted_iota(jnp.int32, (1, EXT), 1)
    column = (place - ROWS) % HALO
    low = (place >= ROWS) & (place < ROWS + EDGE)
    high = (place >= ROWS + SENT) & (place < ROWS + SENT + EDGE)
    usable = (
        (place < ROWS)
        | (low & (HALO - column <= band_ref[0, 0]))
        | (high & (column + 1 <= band_ref[0, 1]))
    )
    scale = HD ** (-0.5)
    scores = jnp.where(usable, dot(queries, keys, OVER_COLS) * scale, -jnp.inf)
    exp_scores = jnp.exp(scores - jnp.max(scores, axis=-1, keepdims=True))
    probs = exp_scores / jnp.sum(exp_scores, axis=-1, keepdims=True)
    probs_low = probs.astype(BF16)
    attended = dot(probs_low, values).astype(BF16)
    d_probs = dot(d_att, values, OVER_COLS)
    inner = jnp.sum(probs * d_probs, axis=-1, keepdims=True)
    d_scores = (probs * (d_probs - inner) * scale).astype(BF16)
    d_query = dot(d_scores, keys)
    d_keys = dot(d_scores, queries, OVER_ROWS)
    d_values = dot(probs_low, d_att, OVER_ROWS)
    own_grads_ref[:, :HD] = d_query
    own_grads_ref[:, HD : 2 * HD] = d_keys[:ROWS]
    own_grads_ref[:, 2 * HD :] = d_values[:ROWS]
    filler = jnp.zeros((PAD - SENT, HD), F32)
    for ref, start in ((low_back_ref, ROWS), (high_back_ref, ROWS + SENT)):
        for place, value in enumerate((d_keys, d_values)):
            rows = jnp.concatenate([value[start : start + SENT], filler], axis=0)
            ref[:, place * HD : (place + 1) * HD] = rows.astype(BF16)
    d_query_ext = jnp.concatenate([d_query, jnp.zeros((2 * SENT, HD), F32)], axis=0)
    left_qkv = jnp.concatenate([d_query_ext.T, d_keys.T, d_values.T], axis=0).astype(BF16)
    left_out = attended.astype(F32).T.astype(BF16)
    left_qkv_ref[...] = left_qkv
    left_out_ref[...] = left_out
    store_grads(
        away_first_ref, away_rest_ref, left_qkv, left_out, normed_refs, cot_ref, x, 1 - core
    )


def own_half_kernel(place_ref, left_qkv_ref, left_out_ref, *refs):
    normed_refs, cot_ref, first_ref, rest_ref = refs[:3], refs[3], refs[4], refs[5]
    store_grads(
        first_ref,
        rest_ref,
        left_qkv_ref[...],
        left_out_ref[...],
        normed_refs,
        cot_ref,
        place_ref[0],
        place_ref[1],
    )


def spread_kernel(place_ref, w_qkv_ref, w_out_ref, out_ref, qkv_block, out_block, sems):
    copies = [
        pltpu.make_async_copy(w_qkv_ref, qkv_block, sems.at[0]),
        pltpu.make_async_copy(w_out_ref, out_block, sems.at[1]),
    ]
    for copy in copies:
        copy.start()
    for copy in copies:
        copy.wait()
    columns = [qkv_block[:, group * HD : (group + 1) * HD] for group in range(3)]
    mine = pick(columns + [out_block[...]], place_ref[0])
    for block in range(BLOCKS):
        out_ref[block] = mine


def piece_kernel(pieces_ref, out_ref):
    total = pieces_ref[0].astype(F32)
    for source in range(1, pieces_ref.shape[0]):
        total = total + pieces_ref[source].astype(F32)
    total = total.astype(BF16)
    for target in range(out_ref.shape[0]):
        out_ref[target] = total


def final_kernel(full_ref, qkv_ref, out_ref):
    for group in range(GROUPS):
        value = jnp.concatenate(
            [
                full_ref[4 * quarter + (group - 2 * inner_line(quarter)) % GROUPS].astype(F32)
                for quarter in range(4)
            ],
            axis=0,
        )
        if group < 3:
            qkv_ref[:, group * HD : (group + 1) * HD] = value.T
        else:
            out_ref[...] = value


def line_kernel(*refs):
    for block in range(BLOCKS):
        total = refs[0][block].astype(F32)
        for ref in refs[1:-1]:
            total = total + ref[block].astype(F32)
        total = total.astype(BF16)
        for quarter in range(4):
            refs[-1][quarter, block] = total[quarter * 32 : (quarter + 1) * 32]


def tokens_kernel(
    place_ref, grads_ref, from_left_ref, from_right_ref, tokens_ref, inverse_ref, *refs
):
    own, other = refs[:GROUPS], refs[GROUPS : 2 * GROUPS]
    out_ref, d_normed, d_qkv = refs[2 * GROUPS :]
    x = place_ref[0]
    core = place_ref[1]
    first, last = edge_chooser((ROWS, PAD), 0)
    d_kv = (
        grads_ref[:, HD:]
        + dot(as_weights(first), from_left_ref[...])
        + dot(as_weights(last), from_right_ref[...])
    )
    d_qkv[0] = grads_ref[:, :HD].astype(BF16)
    d_qkv[1] = d_kv[:, :HD].astype(BF16)
    d_qkv[2] = d_kv[:, HD:].astype(BF16)
    d_qkv[3] = jnp.zeros((ROWS, HD), BF16)
    left = jnp.concatenate(
        [d_qkv[(x - step + GROUPS) % GROUPS] for step in range(GROUPS)], axis=1
    )
    total = jnp.zeros((ROWS, HD), F32)
    for parts, side in ((own, core), (other, 1 - core)):
        for block in range(BLOCKS):
            weights = jnp.concatenate([part[block] for part in parts], axis=1)
            piece = dot(left, weights, OVER_COLS)
            columns = feature_block(block, side)
            d_normed[:, columns] = piece
            total = total + piece * tokens_ref[:, columns].astype(F32)
    inverse = inverse_ref[...]
    mean = jnp.sum(total, axis=-1, keepdims=True) * (1.0 / (2 * BLOCKS * HD))
    factor = inverse * inverse * inverse * mean
    for block in range(2 * BLOCKS):
        columns = slice(block * HD, (block + 1) * HD)
        out_ref[:, columns] = (
            inverse * d_normed[:, columns] - tokens_ref[:, columns].astype(F32) * factor
        ).astype(BF16)


def call(body, operands, outs, scratch, flops, in_bytes, smem):
    whole = pl.BlockSpec(memory_space=pltpu.VMEM)
    scalars = pl.BlockSpec(memory_space=pltpu.SMEM)
    return pl.pallas_call(
        body,
        in_specs=[scalars] * smem + [whole] * (len(operands) - smem),
        out_specs=[whole] * len(outs),
        out_shape=[jax.ShapeDtypeStruct(shape, dtype) for shape, dtype in outs],
        scratch_shapes=[pltpu.VMEM(shape, dtype) for shape, dtype in scratch],
        compiler_params=pltpu.CompilerParams(vmem_limit_bytes=VMEM_BYTES),
        cost_estimate=pl.CostEstimate(
            flops=flops, bytes_accessed=in_bytes, transcendentals=0
        ),
    )(*operands)


def inner_line(zlo):
    return (zlo + 1) // 2 % 2


def send(value, step):
    if step == 2:
        return lax.ppermute(value, "zlo", [(0, 1), (1, 0), (2, 3), (3, 2)])
    return lax.ppermute(value, "x", shift_pairs(GROUPS, step))


def line_groups():
    return [
        [
            (((held - 2 * inner_line(zlo)) % GROUPS * 8 + y) * 4 + zlo) * 2 + zhi
            for zlo in range(4)
            for zhi in range(2)
            for y in range(8)
        ]
        for held in range(GROUPS)
    ]


def mirrored_groups():
    return [
        [y * 8 + (3 - zlo if zhi else zlo) * 2 + zhi for zhi in range(2) for y in range(8)]
        for zlo in range(4)
    ]


def local(tokens, w_qkv, w_out, band, cotangent):
    samples, lat_rows, lon_cols, features = tokens.shape
    held = (lax.axis_index("x") + 2 * inner_line(lax.axis_index("zlo"))) % GROUPS
    place = jnp.stack([held, lax.axis_index("core")]).astype(jnp.int32)
    forward = shift_pairs(16, 1)
    backward = shift_pairs(16, -1)
    swap = shift_pairs(2, 1)
    tok_rows = tokens.reshape(ROWS, features)
    cot_rows = cotangent.reshape(ROWS, features)
    spread = pl.pallas_call(
        spread_kernel,
        in_specs=[
            pl.BlockSpec(memory_space=pltpu.SMEM),
            pl.BlockSpec(memory_space=pl.ANY),
            pl.BlockSpec(memory_space=pl.ANY),
        ],
        out_specs=pl.BlockSpec(memory_space=pltpu.VMEM),
        out_shape=jax.ShapeDtypeStruct((BLOCKS, HD, HD), BF16),
        scratch_shapes=[
            pltpu.VMEM((HD, 3 * HD), BF16),
            pltpu.VMEM((HD, HD), BF16),
            pltpu.SemaphoreType.DMA((2,)),
        ],
        compiler_params=pltpu.CompilerParams(vmem_limit_bytes=VMEM_BYTES),
        cost_estimate=pl.CostEstimate(flops=0, bytes_accessed=700_000, transcendentals=0),
    )(place, w_qkv, w_out)
    spread = lax.all_to_all(
        spread, ("y", "zlo", "zhi"), 0, 0, axis_index_groups=mirrored_groups()
    )
    steps = {step: send(spread, step) for step in STEPS}
    own = [spread, steps[1], steps[2], steps[3]]
    passed = lax.ppermute(spread, "core", swap)
    late_rows, passed = lax.optimization_barrier((tok_rows, passed))
    normed_own, inverse, first, last = call(
        normalise_kernel,
        [late_rows],
        [
            ((ROWS, features), BF16),
            ((ROWS, 1), F32),
            ((SENT, features), BF16),
            ((SENT, features), BF16),
        ],
        [],
        200_000_000,
        3_000_000,
        0,
    )
    low = lax.ppermute(last, TILE, forward)
    high = lax.ppermute(first, TILE, backward)
    own[3], low, high = lax.optimization_barrier((own[3], low, high))
    normed = [normed_own, low, high]
    other = [passed] + [lax.ppermute(part, "core", swap) for part in own[1:]]

    first_shape = ((BLOCKS, HD, HD), BF16)
    rest_shape = ((GROUPS - 1, BLOCKS, HD, HD), BF16)
    away_first, away_rest, left_qkv, left_out, own_grads, low_back, high_back = call(
        attention_kernel,
        [place, band, *normed, cot_rows, *own, *other],
        [
            first_shape,
            rest_shape,
            ((3 * HD, EXT), BF16),
            ((HD, ROWS), BF16),
            ((ROWS, 3 * HD), F32),
            ((PAD, 2 * HD), BF16),
            ((PAD, 2 * HD), BF16),
        ],
        [((EXT, 3 * HD), BF16), ((ROWS, HD), BF16)],
        3_000_000_000,
        12_000_000,
        2,
    )
    got_rest = lax.ppermute(away_rest, "core", swap)
    got_first = lax.ppermute(away_first, "core", swap)
    kept_first, kept_rest = call(
        own_half_kernel,
        [place, left_qkv, left_out, *normed, cot_rows],
        [first_shape, rest_shape],
        [],
        500_000_000,
        6_000_000,
        1,
    )
    sent = [
        (kept_rest[step].astype(F32) + got_rest[step].astype(F32)).astype(BF16)
        for step in range(GROUPS - 1)
    ]
    arrived = [
        send(sent[step - 1], step) for step in STEPS
    ]
    from_right = lax.ppermute(low_back, TILE, backward)
    from_left = lax.ppermute(high_back, TILE, forward)
    (line,) = call(
        line_kernel,
        [kept_first, got_first, *arrived],
        [((4, BLOCKS, 32, HD), BF16)],
        [],
        2_000_000,
        3_000_000,
        0,
    )
    line, from_left, from_right = lax.optimization_barrier((line, from_left, from_right))
    pieces = lax.all_to_all(
        line.reshape(64, 32, HD),
        ("x", "y", "zlo", "zhi"),
        0,
        0,
        axis_index_groups=line_groups(),
    )
    (d_tokens,) = call(
        tokens_kernel,
        [place, own_grads, from_left, from_right, tok_rows, inverse, *own, *other],
        [((ROWS, features), BF16)],
        [((ROWS, features), F32), ((GROUPS, ROWS, HD), BF16)],
        800_000_000,
        8_000_000,
        1,
    )
    pieces, d_tokens = lax.optimization_barrier((pieces, d_tokens))
    (piece,) = call(
        piece_kernel, [pieces], [((16, 32, HD), BF16)], [], 1_000_000, 1_000_000, 0
    )
    full = lax.all_to_all(piece, ("zlo", "x"), 0, 0)
    grad_qkv, grad_out = call(
        final_kernel, [full], [((HD, 3 * HD), F32), ((HD, HD), F32)], [], 1_000_000, 500_000, 0
    )
    return (d_tokens.reshape(tokens.shape), grad_qkv, grad_out)


def solution(mesh):
    inner = jax.sharding.Mesh(
        mesh.devices.reshape(4, 4, 8, 2, 2), ("x", "zlo", "y", "zhi", "core")
    )
    placed = (
        P(FSDP, None, TILE, None),
        P(FSDP, None),
        P(None, FSDP),
        P(TILE, None),
        P(FSDP, None, TILE, None),
    )
    return jax.shard_map(
        local,
        mesh=inner,
        in_specs=placed,
        out_specs=(P(FSDP, None, TILE, None), P(FSDP, None), P(None, FSDP)),
        check_vma=False,
    )
```
